512 devices in a mesh: table: 8 (over y), batch: 64 (over z, x, core).
Axes of the slice: x: 4, y: 8, z: 8, core: 2. Of those that a mesh axis runs over, the one named last changes fastest.
Arguments:
- table: bfloat16 [8192, 512], P('table'), may hold values from -6 to 6
- owner: int32 [131072, 1], P(('table', 'batch')), may hold values from 0 to 7; in each aligned block of 256 rows (0 to 255, 256 to 511, ...) at most 48 rows name the same one
- local_row: int32 [131072], P(('table', 'batch')), may hold values from 0 to 1023
- lengths: int32 [512, 2], P(('table', 'batch')), may hold values from 1 to 192, 256 in all within a row
- w_in: bfloat16 [512, 2048], replicated, may hold values from -0.25 to 0.25
- w_out: bfloat16 [512, 512], replicated, may hold values from -0.25 to 0.25
- cotangent: bfloat16 [131072, 512], P(('table', 'batch')), may hold values from -0.59765625 to 0.59765625
Outputs:
- layer_out: bfloat16 [131072, 512], P(('table', 'batch'))
- table_grad: float32 [8192, 512], P(('table', 'batch'))
- w_out_grad: bfloat16 [512, 512], P('batch')
The draws below stay inside these ranges and needn't reach their ends.
Inputs may be any that keep to these rules, and one draw needn't show every extreme that they name: `owner`: among the rows of one device no shard is named by more than 48 rows, and in every draw some device names some shard exactly 48 times. `lengths`: each row sums to 256; the largest entry of the whole array is 192.
All inputs are finite; a program needn't handle non-finite values.
Results may differ from the reference program's by a relative error of at most 0.017.
Values may be sent and summed in bfloat16 or wider, within the bound.
A program may use at most 64 MiB of HBM per device.

```python
import math
import jax
import jax.numpy as jnp
import numpy as np
from jax import lax

D = 512
HEADS = 8
TOK_DEV = 256
SLOTS = 2
MOST_LEN = 192
ROWS_DEV = 1024
CAP = 48
SHARDS = 512
TOKENS = 131072
ROWS = 8192
N_TABLE = 8


def plant(values, rng, least, high):
    index_at = [jax.random.randint(jax.random.fold_in(rng, axis), (), 0, length) for axis, length in enumerate(values.shape)]
    widest = values.shape.index(max(values.shape))
    neighbour = index_at[:widest] + [(index_at[widest] + 1) % values.shape[widest]] + index_at[widest + 1:]
    return values.at[tuple(index_at)].set(least).at[tuple(neighbour)].set(high)


def block_scale(rng, extent, shards, smallest, largest):
    loudness = 1.0
    for dim, shards_of in shards:
        heights = jax.random.uniform(jax.random.fold_in(jax.random.fold_in(rng, 6), dim), (shards_of,), jnp.float32, smallest / len(shards), largest / len(shards))
        loudness = loudness * jnp.repeat(jnp.exp(heights), extent[dim] // shards_of).reshape((-1,) + (1,) * (len(extent) - 1 - dim))
    return loudness


def rank_bounds(amount, skew):
    portions = [(1 << 20) // math.isqrt(rank ** skew) + 1 for rank in range(1, amount + 1)]
    deviation = 1 + sum(portions) // (1 << 30)
    return np.cumsum(np.array([max(1, weight // deviation) for weight in portions]))


def ranked(rng, extent, amount, slope):
    table = rank_bounds(amount, slope)
    ticket = jax.random.randint(jax.random.fold_in(rng, 1), extent, 0, int(table[amount - 1]))
    grade = jnp.searchsorted(jnp.asarray(table, jnp.int32), ticket, side="right")
    return jax.random.permutation(jax.random.fold_in(rng, 2), amount)[grade].astype(jnp.int32)


def profile(number_of, total, most, skew):
    loads = [(1 << 20) // math.isqrt(grade ** skew) + 1 for grade in range(2, number_of + 1)]
    spare, counts = total - most - (number_of - 1), [1] * (number_of - 1)
    while spare > 0:
        movable = [i for i in range(number_of - 1) if counts[i] < most]
        pool, remaining = sum([loads[i] for i in movable]), spare
        for i in movable:
            extra = min(most - counts[i], max(1, remaining * loads[i] // pool), spare)
            counts[i] = counts[i] + extra
            spare = spare - extra
    return np.array([most] + counts)


def uneven(key, count, total, most, lean):
    if count == 2:
        one = jax.random.randint(key, (), max(1, total - most), min(most, total - 1) + 1)
        return jnp.stack([one, total - one])
    tallies = jnp.asarray(profile(count, total, most, lean), jnp.int32)
    pairs = (count - 1) // 2
    giver, receiver = tallies[1:1 + 2 * pairs:2], tallies[2:2 + 2 * pairs:2]
    room = jnp.minimum(giver - 1, most - receiver)
    shifted = jax.random.randint(jax.random.fold_in(key, 1), (pairs,), 0, 1 << 20) % (room + 1)
    tallies = tallies.at[1:1 + 2 * pairs:2].set(giver - shifted).at[2:2 + 2 * pairs:2].set(receiver + shifted)
    return tallies[jax.random.permutation(jax.random.fold_in(key, 2), count)]


def assign_block(stream_key, own, number, rows, number_of, top, reach, lean):
    ranking = jax.random.permutation(stream_key, number_of)
    crowded, common = portions_of(number_of, rows * top, reach, lean, True), portions_of(number_of, rows * top, reach, lean, False)
    places = jnp.arange(number_of)

    def named(tallies, turn):
        used = int((tallies > 0).sum())
        fixed = max(1, used // 4)
        shifted = fixed + (places - fixed + turn * (used - fixed)) % max(1, number_of - fixed)
        return jnp.zeros((number_of,), jnp.int32).at[ranking[jnp.where(places < fixed, places, shifted)]].set(jnp.asarray(tallies, jnp.int32))

    tallies = jnp.where(number % 4 == 0, named(crowded, number // 4), named(common, number - number // 4 - 1))
    mixed = jax.random.permutation(jax.random.fold_in(own, 3), number_of)
    giver, sink = mixed[0:number_of // 2 * 2:2], mixed[1:number_of // 2 * 2:2]
    room = jnp.minimum(tallies[giver] - 1, reach - tallies[sink]) // 2
    room = jnp.where((giver == ranking[0]) | (sink == ranking[0]) | (tallies[sink] == 0), 0, jnp.maximum(room, 0))
    shifted = jax.random.randint(jax.random.fold_in(own, 4), (number_of // 2,), 0, 1 << 20) % (room + 1)
    tallies = tallies.at[giver].add(-shifted).at[sink].add(shifted)
    items = jnp.searchsorted(jnp.cumsum(tallies), jnp.arange(rows * top), side="right").astype(jnp.int32)
    table = items.reshape(top, rows).T
    table = table[jax.random.permutation(jax.random.fold_in(own, 1), rows)]
    turn = jax.random.randint(jax.random.fold_in(own, 2), (rows, 1), 0, top)
    return jnp.take_along_axis(table, (jnp.arange(top)[None, :] + turn) % top, axis=1)


def portions_of(number_of, total, reach, slope, full):
    loads = [(1 << 20) // math.isqrt(grade ** slope) + 1 for grade in range(1, number_of + 1)]
    largest = reach if full else min(reach, max(-(-total // number_of), total * loads[0] // sum(loads)))
    least = 1 if total - largest >= number_of - 1 else 0
    holding, rest = [largest] + [least] * (number_of - 1), total - largest - least * (number_of - 1)
    while rest > 0:
        movable = [i for i in range(1, number_of) if holding[i] < largest] or [i for i in range(1, number_of) if holding[i] < reach]
        mass, budget = sum([loads[i] for i in movable]), rest
        for i in movable:
            addition = min(reach - holding[i], max(1, budget * loads[i] // mass), rest)
            holding[i] = holding[i] + addition
            rest = rest - addition
    return np.array(holding)


def centred(rng, extent, scale, bound, shards=(), kind=jnp.bfloat16):
    array = scale * jax.random.normal(rng, extent, jnp.float32)
    if shards:
        array = array * block_scale(rng, extent, shards, -0.22, 0.18)
    return jnp.clip(array, -bound, bound).astype(kind)


def setup_inputs(seed: int = 0) -> dict:
    streams_of = jax.random.split(jax.random.key(seed), 8)
    table = centred(streams_of[0], (ROWS, D), 1.0, 6.0, ((0, 8),))
    owner_keys = jax.random.split(jax.random.fold_in(streams_of[1], 1), TOKENS // TOK_DEV)
    owner_turns = jax.random.permutation(jax.random.fold_in(streams_of[1], 3), TOKENS // TOK_DEV)
    owner = jax.vmap(lambda own, number: assign_block(jax.random.fold_in(streams_of[1], 2), own, number, TOK_DEV, N_TABLE, 1, CAP, 2))(owner_keys, owner_turns).reshape((TOKENS, 1))
    local_row = plant(ranked(streams_of[2], (TOKENS,), ROWS_DEV, 1), jax.random.fold_in(streams_of[2], 3), 0, ROWS_DEV - 1).astype(jnp.int32)
    lengths = jax.vmap(lambda own: uneven(own, SLOTS, TOK_DEV, MOST_LEN, 2))(jax.random.split(streams_of[3], SHARDS)).reshape((SHARDS, SLOTS)).astype(jnp.int32)
    w_in = centred(streams_of[4], (D, 4 * D), D ** -0.5, 0.25)
    w_out = centred(streams_of[5], (D, D), D ** -0.5, 0.25)
    cotangent = centred(streams_of[6], (TOKENS, D), 0.1, 0.59765625, ((0, 512),))
    return dict(table=table, owner=owner, local_row=local_row, lengths=lengths, w_in=w_in, w_out=w_out, cotangent=cotangent)


EPSILON = 1e-05

def layer_norm(values):
    center = lax.optimization_barrier(jnp.mean(values, axis=-1, keepdims=True))
    spread = lax.optimization_barrier(jnp.mean((values - center) * (values - center), axis=-1, keepdims=True))
    return (values - center) * lax.rsqrt(spread + EPSILON)

def history_index(length_row, count):
    bounds = jnp.cumsum(length_row)
    places = jnp.arange(count)
    return lax.optimization_barrier(jnp.sum((places[:, None] >= bounds[None, :]).astype(jnp.int32), axis=1))

def hstu_block(embedded, history, w_in, w_out):
    count, width = embedded.shape
    head_size = width // HEADS
    inputs = embedded.astype(jnp.float32)
    normed = layer_norm(inputs).astype(jnp.bfloat16)
    hidden = jnp.dot(normed, w_in, preferred_element_type=jnp.float32)
    branches = jax.nn.silu(hidden).astype(jnp.bfloat16)
    gate_part = branches[:, :width]
    value_part = branches[:, width:2 * width].reshape(count, HEADS, head_size)
    query_part = branches[:, 2 * width:3 * width].reshape(count, HEADS, head_size)
    key_part = branches[:, 3 * width:].reshape(count, HEADS, head_size)
    scores = jnp.einsum('ihe,jhe->hij', query_part.astype(jnp.float32), key_part.astype(jnp.float32)) * head_size ** (-0.5)
    places = jnp.arange(count)
    allowed = (history[:, None] == history[None, :]) & (places[None, :] <= places[:, None])
    weights = jnp.where(allowed[None], jax.nn.silu(scores) / MOST_LEN, 0.0).astype(jnp.bfloat16)
    attended = jnp.einsum('hij,jhe->ihe', weights.astype(jnp.float32), value_part.astype(jnp.float32)).reshape(count, width)
    gated = (layer_norm(attended) * gate_part.astype(jnp.float32)).astype(jnp.bfloat16)
    result = (jnp.dot(gated, w_out, preferred_element_type=jnp.float32) + inputs).astype(jnp.bfloat16)
    return (result, gated)

def reference(table, owner, local_row, lengths, w_in, w_out, cotangent):
    row_index = (owner[:, 0] * ROWS_DEV + local_row).astype(jnp.int32)
    embedded = jnp.take(table, row_index, axis=0)
    blocks = embedded.reshape(SHARDS, TOK_DEV, D)
    cot_blocks = cotangent.reshape(SHARDS, TOK_DEV, D)

    def advance(total, packed):
        block, cot_block, length_row = packed
        history = history_index(length_row, TOK_DEV)
        result, pullback, gated = jax.vjp(lambda values: hstu_block(values, history, w_in, w_out), block, has_aux=True)
        token_grads = pullback(cot_block)[0]
        total = total + jnp.dot(gated.T, cot_block, preferred_element_type=jnp.float32)
        return (total, (result, token_grads))
    start = jnp.zeros((D, D), jnp.float32)
    total, (results, token_grads) = lax.scan(advance, start, (blocks, cot_blocks, lengths))
    table_grad = jnp.zeros((ROWS, D), jnp.float32).at[row_index].add(token_grads.reshape(TOKENS, D).astype(jnp.float32))
    return (results.reshape(TOKENS, D), table_grad, total.astype(jnp.bfloat16))
```

```python
import functools

import jax
import jax.numpy as jnp
from jax import lax
from jax.experimental import pallas as pl
from jax.experimental.pallas import tpu as pltpu
from jax.sharding import PartitionSpec as P

HEADS = 8
MOST_LEN = 192
EPSILON = 1e-05
CORES = 2
F32 = jnp.float32
BF16 = jnp.bfloat16


def dot(a, b):
    return lax.dot_general(a, b, (((1,), (0,)), ((), ())), preferred_element_type=F32)


def dot_nt(a, b):
    return lax.dot_general(a, b, (((1,), (1,)), ((), ())), preferred_element_type=F32)


def dot_tn(a, b):
    return lax.dot_general(a, b, (((0,), (0,)), ((), ())), preferred_element_type=F32)


def iota(shape, dim):
    return lax.broadcasted_iota(jnp.int32, shape, dim)


def sigmoid(z):
    return 0.5 * jnp.tanh(0.5 * z) + 0.5


def far_first(n):
    return sorted(range(n), key=lambda d: -min(d, n - d))


def kernel(
    ny, nz, nx, cap,
    owner_hbm, row_hbm, len_hbm, table_hbm, w_in_hbm, w_out_hbm, cot_hbm,
    out_hbm, tgrad_ref, wgrad_ref,
    owner_ref, row_ref, len_ref, table, w_in, w_out, cot, out,
    idx_own, idx_all, reply, fetched, place, hot,
    branch, slope, weight, sslope, sides,
    packed, ret, half_out, half_in, rs_out, rs_in,
    wsw_out, wsw_in, wrs_out, wrs_in, way_out, way_in, wfin_out, wfin_in,
    load_sem, store_sem, send_sem, recv_sem,
):
    tok, width = cot.shape
    nc = CORES
    pair_width = 128
    pairs = width // pair_width
    chunk = width // nx
    half_width = width // nc
    slots = ny * cap
    listed_width = idx_own.shape[-1]
    y = lax.axis_index("table")
    b = lax.axis_index("batch")
    core = b % nc
    x = (b // nc) % nx
    z = b // (nc * nx)
    zx = z * nx + x
    sibling = {"table": y, "batch": zx * nc + (1 - core)}

    def device(yy, zz, xx):
        return {"table": yy, "batch": (zz * nx + xx) * nc + core}

    columns = [(dy, dx) for dy in far_first(ny) for dx in far_first(nx) if (dy, dx) != (0, 0)]
    planes = [(dz, dx) for dz in far_first(nz) for dx in far_first(nx) if (dz, dx) != (0, 0)]

    def in_column(dy, dx):
        return (y + dy) & (ny - 1), (x + dx) & (nx - 1)

    def in_plane(dz, dx):
        return (z + dz) & (nz - 1), (x + dx) & (nx - 1)

    barrier = pltpu.get_barrier_semaphore()
    greeted = 0
    for dy, dx in columns:
        yy, xx = in_column(dy, dx)
        pl.semaphore_signal(barrier, inc=1, device_id=device(yy, z, xx))
        greeted += 1
    for dz, dx in planes:
        if dz == 0:
            continue
        zz, xx = in_plane(dz, dx)
        pl.semaphore_signal(barrier, inc=1, device_id=device(y, zz, xx))
        greeted += 1
    pl.semaphore_signal(barrier, inc=1, device_id=sibling)
    greeted += 1

    loads = [
        pltpu.make_async_copy(src, dst, load_sem.at[i])
        for i, (src, dst) in enumerate(
            [
                (owner_hbm, owner_ref),
                (row_hbm, row_ref),
                (table_hbm, table),
                (len_hbm, len_ref),
                (cot_hbm, cot),
                (w_out_hbm, w_out),
                (w_in_hbm, w_in),
            ]
        )
    ]
    for load in loads:
        load.start()

    loads[0].wait()
    loads[1].wait()
    owner = owner_ref[...]
    rows = row_ref[...]
    mine = (iota((ny, tok), 0) == owner).astype(F32)
    earlier = (iota((tok, tok), 0) < iota((tok, tok), 1)).astype(F32).astype(BF16)
    before = dot(mine.astype(BF16), earlier)
    rank = jnp.sum(mine * before, axis=0, keepdims=True).astype(jnp.int32)
    rank_hot = (iota((listed_width, tok), 0) == rank).astype(F32).astype(BF16)
    high = (rows // 32).astype(F32)
    low = (rows % 32).astype(F32)
    parts = jnp.concatenate([mine * high, mine * low], axis=0).astype(BF16)
    listed = dot_nt(parts, rank_hot)
    listed = (listed[:ny] * 32.0 + listed[ny:]).astype(jnp.int32)
    for o in range(ny):
        idx_own[o] = listed[o : o + 1]
    idx_all[x * ny + y] = idx_own[y]
    slot = owner * cap + rank
    place[...] = (iota((slots, tok), 0) == slot).astype(F32).astype(BF16)
    slot_col = jnp.broadcast_to(slot.astype(F32), (8, tok)).T[:, :1].astype(jnp.int32)
    unplace = (iota((tok, slots), 1) == slot_col).astype(F32).astype(BF16)

    pl.semaphore_wait(barrier, greeted)

    def send(src, dst, stage, target):
        copy = pltpu.make_async_remote_copy(
            src_ref=src,
            dst_ref=dst,
            send_sem=send_sem.at[stage],
            recv_sem=recv_sem.at[stage],
            device_id=target,
        )
        copy.start()

    def wait_recv(slab, stage):
        pltpu.make_async_copy(slab, slab, recv_sem.at[stage]).wait()

    def wait_send(slab, stage):
        pltpu.make_async_copy(slab, slab, send_sem.at[stage]).wait()

    near = [dy for dy in far_first(ny) if dy]
    for dy in near:
        yy, _ = in_column(dy, 0)
        send(idx_own.at[yy], idx_all.at[x * ny + y], 0, device(yy, z, x))
    loads[2].wait()
    wait_recv(idx_all.at[pl.ds(0, ny - 1)], 0)

    order = far_first(ny)
    asked = [idx_all[x * ny + ((y + dy) & (ny - 1))] for dy in order]
    if ny < 8:
        asked = asked + [asked[0]] * (8 - ny)
    asked = jnp.concatenate(asked, axis=0).astype(F32).T.astype(jnp.int32)
    shard_rows = table.shape[0]
    group = 2
    for g in range(0, ny, group):
        picks = jnp.concatenate(
            [iota((cap, shard_rows), 1) == asked[:cap, k : k + 1] for k in range(g, g + group)], axis=0
        )
        found = dot(picks.astype(F32).astype(BF16), table[...]).astype(BF16)
        for k in range(g, g + group):
            dy = order[k]
            block = found[(k - g) * cap : (k - g + 1) * cap]
            if dy == 0:
                fetched[y] = block
            else:
                reply[k] = block
                yy, _ = in_column(dy, 0)
                send(reply.at[k], fetched.at[y], 2, device(yy, z, x))

    for dy, dx in columns:
        if dx == 0:
            continue
        yy, xx = in_column(dy, dx)
        send(idx_own.at[yy], idx_all.at[x * ny + y], 1, device(yy, z, xx))

    loads[3].wait()
    loads[4].wait()
    loads[5].wait()
    dg = dot_nt(cot[...], w_out[...]).astype(BF16).astype(F32)
    bound = len_ref[:, :1]
    place_i = iota((tok, tok), 0)
    place_j = iota((tok, tok), 1)
    allowed = ((place_i >= bound) == (place_j >= bound)) & (place_j <= place_i)
    mask = jnp.where(allowed, 1.0 / MOST_LEN, 0.0).astype(F32)
    wait_recv(idx_all.at[pl.ds(0, (nx - 1) * ny)], 1)
    half_rows = shard_rows // nc
    for s in range(2):
        side = 1 - core if s == 0 else core
        m = iota((half_rows, cap), 0)
        row_at = (m // 16) * 32 + side * 16 + m % 16
        for k in range(nx * ny):
            hot[s, :, k * cap : (k + 1) * cap] = (
                (row_at == idx_all[k][:, :cap]).astype(F32).astype(BF16)
            )
    loads[6].wait()

    wait_recv(fetched.at[pl.ds(0, ny - 1)], 2)

    embedded = dot(unplace, fetched[...].reshape(slots, width)).astype(BF16)
    embedded = embedded.astype(F32)
    center = jnp.mean(embedded, axis=-1, keepdims=True)
    shifted = embedded - center
    scale = lax.rsqrt(jnp.mean(shifted * shifted, axis=-1, keepdims=True) + EPSILON)
    normed = shifted * scale
    normed_b = normed.astype(BF16)
    for i in range(4):
        hidden = dot(normed_b, w_in[:, i * width : (i + 1) * width])
        sig = sigmoid(hidden)
        value = hidden * sig
        branch[i] = value.astype(BF16)
        slope[i] = sig + value * (1.0 - sig)

    first_lane = iota((tok, pair_width), 1) < width // HEADS
    halves = [(0, tok // 2, tok // 2), (tok // 2, tok, tok)]

    def split(values):
        zero = jnp.zeros_like(values)
        return jnp.where(first_lane, values, zero), jnp.where(first_lane, zero, values)

    attended = []
    for p in range(pairs):
        lanes = slice(p * pair_width, (p + 1) * pair_width)
        v = split(branch[1, :, lanes])
        q = split(branch[2, :, lanes] * BF16(0.125))
        k = branch[3, :, lanes]
        result = []
        for lo, hi, js in halves:
            total = None
            for h in range(2):
                score = dot_nt(q[h][lo:hi], k[:js])
                sig = sigmoid(score)
                value = score * sig
                m = mask[lo:hi, :js]
                w = (value * m).astype(BF16)
                weight[2 * p + h, lo:hi, :js] = w
                sslope[2 * p + h, lo:hi, :js] = (sig + value * (1.0 - sig)) * m
                term = dot(w, v[h][:js])
                total = term if total is None else total + term
            result.append(total)
        attended.append(jnp.concatenate(result, axis=0))
    attended = jnp.concatenate(attended, axis=1)
    center2 = jnp.mean(attended, axis=-1, keepdims=True)
    shifted2 = attended - center2
    scale2 = lax.rsqrt(jnp.mean(shifted2 * shifted2, axis=-1, keepdims=True) + EPSILON)
    normed2 = shifted2 * scale2
    gate = branch[0].astype(F32)
    gated = (normed2 * gate).astype(BF16)

    wgrad = dot_tn(gated, cot[...])
    wgrad = [wgrad[:, c * half_width : (c + 1) * half_width] for c in range(2)]
    wsw_out[...] = jnp.where(core == 0, wgrad[1], wgrad[0]).astype(BF16)
    wown = jnp.where(core == 0, wgrad[0], wgrad[1])
    send(wsw_out, wsw_in, 3, sibling)

    out[...] = (dot(gated, w_out[...]) + embedded).astype(BF16)
    store = pltpu.make_async_copy(out, out_hbm, store_sem)
    store.start()

    d_n2 = dg * gate
    d_gate = (dg * normed2).astype(BF16).astype(F32)
    d_att = scale2 * (
        d_n2
        - jnp.mean(d_n2, axis=-1, keepdims=True)
        - normed2 * jnp.mean(d_n2 * normed2, axis=-1, keepdims=True)
    )
    d_att = d_att.astype(BF16)
    d_normed = dot_nt((d_gate * slope[0]).astype(BF16), w_in[:, :width])

    for p in range(pairs):
        lanes = slice(p * pair_width, (p + 1) * pair_width)
        if p == 1:
            wait_recv(wsw_in, 3)
            wblock = wown.shape[0] // (nz * nx)
            wrs_out[...] = (wown + wsw_in[...].astype(F32)).astype(BF16).reshape(nz * nx, wblock, half_width)
            wrs_in[zx] = wrs_out[zx]
            for dz, dx in planes:
                zz, xx = in_plane(dz, dx)
                send(wrs_out.at[zz * nx + xx], wrs_in.at[zx], 4, device(y, zz, xx))
        d_o = split(d_att[:, lanes])
        q = split(branch[2, :, lanes] * BF16(0.125))
        k = split(branch[3, :, lanes])
        v = branch[1, :, lanes]
        half = tok // 2
        dv_low = dv_all = dk_low = dk_all = None
        dq = []
        for lo, hi, js in halves:
            dq_sum = None
            for h in range(2):
                d_w = dot_nt(d_o[h][lo:hi], v[:js])
                d_s = (d_w * sslope[2 * p + h, lo:hi, :js]).astype(BF16)
                term = dot(d_s, k[h][:js])
                dq_sum = term if dq_sum is None else dq_sum + term
                dk = dot_tn(d_s, q[h][lo:hi])
                dv = dot_tn(weight[2 * p + h, lo:hi, :js], d_o[h][lo:hi])
                if lo == 0:
                    dk_low = dk if dk_low is None else dk_low + dk
                    dv_low = dv if dv_low is None else dv_low + dv
                else:
                    dk_all = dk if dk_all is None else dk_all + dk
                    dv_all = dv if dv_all is None else dv_all + dv
            dq.append(dq_sum * 0.125)
        dq = jnp.concatenate(dq, axis=0)
        dk = jnp.concatenate([dk_all[:half] + dk_low, dk_all[half:]], axis=0)
        dv = jnp.concatenate([dv_all[:half] + dv_low, dv_all[half:]], axis=0)
        for i, value in ((1, dv), (2, dq), (3, dk)):
            value = value.astype(BF16).astype(F32)
            sides[i - 1, :, lanes] = (value * slope[i, :, lanes]).astype(BF16)

    for i in range(1, 4):
        d_normed = d_normed + dot_nt(sides[i - 1], w_in[:, i * width : (i + 1) * width])
    d_normed = d_normed.astype(BF16).astype(F32)
    d_emb = scale * (
        d_normed
        - jnp.mean(d_normed, axis=-1, keepdims=True)
        - normed * jnp.mean(d_normed * normed, axis=-1, keepdims=True)
    )
    token_grads = (d_emb + cot[...].astype(F32)).astype(BF16)

    spread = dot(place[...], token_grads).astype(BF16)
    for xx in range(nx):
        packed[xx] = spread[:, xx * chunk : (xx + 1) * chunk].reshape(ny, cap, chunk)
    ret[x * ny + y] = packed[x, y]
    for dy, dx in columns:
        yy, xx = in_column(dy, dx)
        send(packed.at[xx, yy], ret.at[x * ny + y], 6, device(yy, z, xx))

    wait_recv(wrs_in.at[pl.ds(0, nz * nx - 1)], 4)
    wsum = jnp.sum(wrs_in[...].astype(F32), axis=0)
    way_out[...] = wsum.astype(BF16)

    wait_recv(ret.at[pl.ds(0, nx * ny - 1)], 6)
    way_in[y] = way_out[...]
    for dy in near:
        yy, _ = in_column(dy, 0)
        send(way_out, way_in.at[y], 5, device(yy, z, x))
    returned = ret[...].reshape(nx * slots, chunk)
    half_out[...] = dot(hot[0], returned).astype(BF16)
    send(half_out, half_in, 8, sibling)
    own_half = dot(hot[1], returned)
    wait_recv(half_in, 8)
    total = own_half + half_in[...].astype(F32)

    rs_out[...] = total.astype(BF16).reshape(nz * nx, 16, chunk)
    rs_in[zx] = rs_out[zx]
    for dz, dx in planes:
        zz, xx = in_plane(dz, dx)
        send(rs_out.at[zz * nx + xx], rs_in.at[zx], 9, device(y, zz, xx))

    wait_recv(way_in.at[pl.ds(0, ny - 1)], 5)
    wsum = jnp.sum(way_in[...].astype(F32), axis=0)
    wrows = wblock // nc
    wsum = [wsum[c * wrows : (c + 1) * wrows] for c in range(2)]
    wfin_out[...] = jnp.where(core == 0, wsum[1], wsum[0])
    wown = jnp.where(core == 0, wsum[0], wsum[1])
    send(wfin_out, wfin_in, 7, sibling)

    wait_recv(wfin_in, 7)
    wother = wfin_in[...]
    wgrad_ref[:, :half_width] = jnp.where(core == 0, wown, wother).astype(BF16)
    wgrad_ref[:, half_width:] = jnp.where(core == 0, wother, wown).astype(BF16)
    wait_send(idx_own.at[pl.ds(0, ny - 1)], 0)
    wait_send(idx_all.at[pl.ds(0, (nx - 1) * ny)], 1)
    wait_send(fetched.at[pl.ds(0, ny - 1)], 2)
    wait_send(wsw_out, 3)
    wait_send(wrs_out.at[pl.ds(0, nz * nx - 1)], 4)
    wait_send(way_in.at[pl.ds(0, ny - 1)], 5)
    wait_send(ret.at[pl.ds(0, nx * ny - 1)], 6)
    wait_send(wfin_out, 7)
    wait_send(half_out, 8)
    store.wait()
    wait_recv(rs_in.at[pl.ds(0, nz * nx - 1)], 9)
    for xx in range(nx):
        acc = None
        for zz in range(nz):
            term = rs_in[zz * nx + xx].astype(F32)
            acc = term if acc is None else acc + term
        tgrad_ref[:, xx * chunk : (xx + 1) * chunk] = acc
    wait_send(rs_out.at[pl.ds(0, nz * nx - 1)], 9)


def hand_on(*refs):
    sems = refs[-1]
    copies = [pltpu.make_async_copy(refs[i], refs[3 + i], sems.at[i]) for i in range(3)]
    for copy in copies:
        copy.start()
    for copy in copies:
        copy.wait()


def on_device(ny, nz, nx, cap, table, owner, local_row, lengths, w_in, w_out, cotangent):
    tok, width = cotangent.shape
    shard_rows = table.shape[0]
    chunk = width // nx
    slots = ny * cap
    nc = CORES
    wblock = width // (nz * nx)
    half_width = width // nc
    vmem = pl.BlockSpec(memory_space=pltpu.VMEM)
    anywhere = pl.BlockSpec(memory_space=pl.ANY)
    V = pltpu.VMEM
    scratch = [
        V((1, tok), jnp.int32),
        V((1, tok), jnp.int32),
        V(lengths.shape, jnp.int32),
        V(table.shape, BF16),
        V(w_in.shape, BF16),
        V(w_out.shape, BF16),
        V(cotangent.shape, BF16),
        V(cotangent.shape, BF16),
        V((ny, 1, -(-cap // 128) * 128), jnp.int32),
        V((nx * ny, 1, -(-cap // 128) * 128), jnp.int32),
        V((ny, cap, width), BF16),
        V((ny, cap, width), BF16),
        V((slots, tok), BF16),
        V((2, shard_rows // nc, nx * slots), BF16),
        V((4, tok, width), BF16),
        V((4, tok, width), F32),
        V((HEADS, tok, tok), BF16),
        V((HEADS, tok, tok), F32),
        V((3, tok, width), BF16),
        V((nx, ny, cap, chunk), BF16),
        V((nx * ny, cap, chunk), BF16),
        V((shard_rows // nc, chunk), BF16),
        V((shard_rows // nc, chunk), BF16),
        V((nz * nx, 16, chunk), BF16),
        V((nz * nx, 16, chunk), BF16),
        V((width, half_width), BF16),
        V((width, half_width), BF16),
        V((nz * nx, wblock, half_width), BF16),
        V((nz * nx, wblock, half_width), BF16),
        V((wblock, half_width), BF16),
        V((ny, wblock, half_width), BF16),
        V((wblock // nc, half_width), F32),
        V((wblock // nc, half_width), F32),
        pltpu.SemaphoreType.DMA((7,)),
        pltpu.SemaphoreType.DMA,
        pltpu.SemaphoreType.DMA((10,)),
        pltpu.SemaphoreType.DMA((10,)),
    ]
    results = pl.pallas_call(
        functools.partial(kernel, ny, nz, nx, cap),
        out_shape=(
            jax.ShapeDtypeStruct((tok, width), BF16),
            jax.ShapeDtypeStruct((shard_rows // (nz * nx * nc), width), F32),
            jax.ShapeDtypeStruct((wblock // nc, width), BF16),
        ),
        in_specs=[anywhere] * 7,
        out_specs=(anywhere, vmem, vmem),
        scratch_shapes=scratch,
        compiler_params=pltpu.CompilerParams(
            collective_id=0, has_side_effects=True, vmem_limit_bytes=56 * 1024 * 1024
        ),
        name="hstu",
    )(
        owner.reshape(1, tok),
        local_row.reshape(1, tok),
        lengths,
        table,
        w_in,
        w_out,
        cotangent,
    )
    return pl.pallas_call(
        hand_on,
        out_shape=tuple(jax.ShapeDtypeStruct(r.shape, r.dtype) for r in results),
        in_specs=[anywhere] * 3,
        out_specs=(anywhere,) * 3,
        scratch_shapes=[pltpu.SemaphoreType.DMA((3,))],
        name="hand_on",
    )(*results)


def build(mesh, nx, cap):
    ny = mesh.shape["table"]
    nz = mesh.shape["batch"] // (nx * CORES)
    return jax.shard_map(
        functools.partial(on_device, ny, nz, nx, cap),
        mesh=mesh,
        in_specs=(
            P("table", None),
            P(("table", "batch"), None),
            P(("table", "batch")),
            P(("table", "batch"), None),
            P(),
            P(),
            P(("table", "batch"), None),
        ),
        out_specs=(P(("table", "batch"), None), P(("table", "batch"), None), P("batch", None)),
        check_vma=False,
    )


def solution(mesh):
    return build(mesh, 4, 48)
```

```python
import functools

import jax
import jax.numpy as jnp
from jax import lax
from jax.experimental import pallas as pl
from jax.experimental.pallas import tpu as pltpu
from jax.sharding import PartitionSpec as P

HEADS = 8
MOST_LEN = 192
EPSILON = 1e-05
CORES = 2
F32 = jnp.float32
BF16 = jnp.bfloat16


def dot(a, b):
    return lax.dot_general(a, b, (((1,), (0,)), ((), ())), preferred_element_type=F32)


def dot_nt(a, b):
    return lax.dot_general(a, b, (((1,), (1,)), ((), ())), preferred_element_type=F32)


def dot_tn(a, b):
    return lax.dot_general(a, b, (((0,), (0,)), ((), ())), preferred_element_type=F32)


def iota(shape, dim):
    return lax.broadcasted_iota(jnp.int32, shape, dim)


def sigmoid(z):
    return 0.5 * jnp.tanh(0.5 * z) + 0.5


def far_first(n):
    return sorted(range(n), key=lambda d: -min(d, n - d))


def kernel(
    ny, nz, nx, cap,
    owner_hbm, row_hbm, len_hbm, table_hbm, w_in_hbm, w_out_hbm, cot_hbm,
    out_hbm, tgrad_ref, wgrad_ref,
    owner_ref, row_ref, len_ref, table, w_in, w_out, cot, out,
    idx_own, idx_all, reply, fetched, place, hot,
    branch, slope, weight, sslope, sides,
    packed, ret, half_out, half_in, rs_out, rs_in,
    wsw_out, wsw_in, wrs_out, wrs_in, way_out, way_in, wfin_out, wfin_in,
    load_sem, store_sem, send_sem, recv_sem,
):
    tok, width = cot.shape
    nc = CORES
    pair_width = 128
    pairs = width // pair_width
    chunk = width // nx
    half_width = width // nc
    slots = ny * cap
    listed_width = idx_own.shape[-1]
    y = lax.axis_index("table")
    b = lax.axis_index("batch")
    core = b % nc
    x = (b // nc) % nx
    z = b // (nc * nx)
    zx = z * nx + x
    sibling = {"table": y, "batch": zx * nc + (1 - core)}

    def device(yy, zz, xx):
        return {"table": yy, "batch": (zz * nx + xx) * nc + core}

    columns = [(dy, dx) for dy in far_first(ny) for dx in far_first(nx) if (dy, dx) != (0, 0)]
    planes = [(dz, dx) for dz in far_first(nz) for dx in far_first(nx) if (dz, dx) != (0, 0)]

    def in_column(dy, dx):
        return (y + dy) & (ny - 1), (x + dx) & (nx - 1)

    def in_plane(dz, dx):
        return (z + dz) & (nz - 1), (x + dx) & (nx - 1)

    barrier = pltpu.get_barrier_semaphore()
    greeted = 0
    for dy, dx in columns:
        yy, xx = in_column(dy, dx)
        pl.semaphore_signal(barrier, inc=1, device_id=device(yy, z, xx))
        greeted += 1
    for dz, dx in planes:
        if dz == 0:
            continue
        zz, xx = in_plane(dz, dx)
        pl.semaphore_signal(barrier, inc=1, device_id=device(y, zz, xx))
        greeted += 1
    pl.semaphore_signal(barrier, inc=1, device_id=sibling)
    greeted += 1

    loads = [
        pltpu.make_async_copy(src, dst, load_sem.at[i])
        for i, (src, dst) in enumerate(
            [
                (owner_hbm, owner_ref),
                (row_hbm, row_ref),
                (table_hbm, table),
                (len_hbm, len_ref),
                (cot_hbm, cot),
                (w_out_hbm, w_out),
                (w_in_hbm, w_in),
            ]
        )
    ]
    for load in loads:
        load.start()

    loads[0].wait()
    loads[1].wait()
    owner = owner_ref[...]
    rows = row_ref[...]
    mine = (iota((ny, tok), 0) == owner).astype(F32)
    earlier = (iota((tok, tok), 0) < iota((tok, tok), 1)).astype(F32).astype(BF16)
    before = dot(mine.astype(BF16), earlier)
    rank = jnp.sum(mine * before, axis=0, keepdims=True).astype(jnp.int32)
    rank_hot = (iota((listed_width, tok), 0) == rank).astype(F32).astype(BF16)
    high = (rows // 32).astype(F32)
    low = (rows % 32).astype(F32)
    parts = jnp.concatenate([mine * high, mine * low], axis=0).astype(BF16)
    listed = dot_nt(parts, rank_hot)
    listed = (listed[:ny] * 32.0 + listed[ny:]).astype(jnp.int32)
    for o in range(ny):
        idx_own[o] = listed[o : o + 1]
    idx_all[x * ny + y] = idx_own[y]
    slot = owner * cap + rank
    place[...] = (iota((slots, tok), 0) == slot).astype(F32).astype(BF16)
    slot_col = jnp.broadcast_to(slot.astype(F32), (8, tok)).T[:, :1].astype(jnp.int32)
    unplace = (iota((tok, slots), 1) == slot_col).astype(F32).astype(BF16)

    pl.semaphore_wait(barrier, greeted)

    def send(src, dst, stage, target):
        copy = pltpu.make_async_remote_copy(
            src_ref=src,
            dst_ref=dst,
            send_sem=send_sem.at[stage],
            recv_sem=recv_sem.at[stage],
            device_id=target,
        )
        copy.start()

    def wait_recv(slab, stage):
        pltpu.make_async_copy(slab, slab, recv_sem.at[stage]).wait()

    def wait_send(slab, stage):
        pltpu.make_async_copy(slab, slab, send_sem.at[stage]).wait()

    near = [dy for dy in far_first(ny) if dy]
    for dy in near:
        yy, _ = in_column(dy, 0)
        send(idx_own.at[yy], idx_all.at[x * ny + y], 0, device(yy, z, x))
    loads[2].wait()
    wait_recv(idx_all.at[pl.ds(0, ny - 1)], 0)

    order = far_first(ny)
    asked = [idx_all[x * ny + ((y + dy) & (ny - 1))] for dy in order]
    if ny < 8:
        asked = asked + [asked[0]] * (8 - ny)
    asked = jnp.concatenate(asked, axis=0).astype(F32).T.astype(jnp.int32)
    shard_rows = table.shape[0]
    group = 2
    for g in range(0, ny, group):
        picks = jnp.concatenate(
            [iota((cap, shard_rows), 1) == asked[:cap, k : k + 1] for k in range(g, g + group)], axis=0
        )
        found = dot(picks.astype(F32).astype(BF16), table[...]).astype(BF16)
        for k in range(g, g + group):
            dy = order[k]
            block = found[(k - g) * cap : (k - g + 1) * cap]
            if dy == 0:
                fetched[y] = block
            else:
                reply[k] = block
                yy, _ = in_column(dy, 0)
                send(reply.at[k], fetched.at[y], 2, device(yy, z, x))

    for dy, dx in columns:
        if dx == 0:
            continue
        yy, xx = in_column(dy, dx)
        send(idx_own.at[yy], idx_all.at[x * ny + y], 1, device(yy, z, xx))

    loads[3].wait()
    loads[4].wait()
    loads[5].wait()
    dg = dot_nt(cot[...], w_out[...]).astype(BF16).astype(F32)
    bound = len_ref[:, :1]
    place_i = iota((tok, tok), 0)
    place_j = iota((tok, tok), 1)
    allowed = ((place_i >= bound) == (place_j >= bound)) & (place_j <= place_i)
    mask = jnp.where(allowed, 1.0 / MOST_LEN, 0.0).astype(F32)
    loads[6].wait()

    wait_recv(fetched.at[pl.ds(0, ny - 1)], 2)

    embedded = dot(unplace, fetched[...].reshape(slots, width)).astype(BF16)
    embedded = embedded.astype(F32)
    center = jnp.mean(embedded, axis=-1, keepdims=True)
    shifted = embedded - center
    scale = lax.rsqrt(jnp.mean(shifted * shifted, axis=-1, keepdims=True) + EPSILON)
    normed = shifted * scale
    normed_b = normed.astype(BF16)
    for i in range(4):
        hidden = dot(normed_b, w_in[:, i * width : (i + 1) * width])
        sig = sigmoid(hidden)
        value = hidden * sig
        branch[i] = value.astype(BF16)
        slope[i] = sig + value * (1.0 - sig)

    first_lane = iota((tok, pair_width), 1) < width // HEADS
    halves = [(0, tok // 2, tok // 2), (tok // 2, tok, tok)]

    def split(values):
        zero = jnp.zeros_like(values)
        return jnp.where(first_lane, values, zero), jnp.where(first_lane, zero, values)

    attended = []
    for p in range(pairs):
        lanes = slice(p * pair_width, (p + 1) * pair_width)
        v = split(branch[1, :, lanes])
        q = split(branch[2, :, lanes] * BF16(0.125))
        k = branch[3, :, lanes]
        result = []
        for lo, hi, js in halves:
            total = None
            for h in range(2):
                score = dot_nt(q[h][lo:hi], k[:js])
                sig = sigmoid(score)
                value = score * sig
                m = mask[lo:hi, :js]
                w = (value * m).astype(BF16)
                weight[2 * p + h, lo:hi, :js] = w
                sslope[2 * p + h, lo:hi, :js] = (sig + value * (1.0 - sig)) * m
                term = dot(w, v[h][:js])
                total = term if total is None else total + term
            result.append(total)
        attended.append(jnp.concatenate(result, axis=0))
    attended = jnp.concatenate(attended, axis=1)
    center2 = jnp.mean(attended, axis=-1, keepdims=True)
    shifted2 = attended - center2
    scale2 = lax.rsqrt(jnp.mean(shifted2 * shifted2, axis=-1, keepdims=True) + EPSILON)
    normed2 = shifted2 * scale2
    gate = branch[0].astype(F32)
    gated = (normed2 * gate).astype(BF16)

    wgrad = dot_tn(gated, cot[...])
    wgrad = [wgrad[:, c * half_width : (c + 1) * half_width] for c in range(2)]
    wsw_out[...] = jnp.where(core == 0, wgrad[1], wgrad[0]).astype(BF16)
    wown = jnp.where(core == 0, wgrad[0], wgrad[1])
    send(wsw_out, wsw_in, 3, sibling)

    out[...] = (dot(gated, w_out[...]) + embedded).astype(BF16)
    store = pltpu.make_async_copy(out, out_hbm, store_sem)
    store.start()

    d_n2 = dg * gate
    d_gate = (dg * normed2).astype(BF16).astype(F32)
    d_att = scale2 * (
        d_n2
        - jnp.mean(d_n2, axis=-1, keepdims=True)
        - normed2 * jnp.mean(d_n2 * normed2, axis=-1, keepdims=True)
    )
    d_att = d_att.astype(BF16)
    d_normed = dot_nt((d_gate * slope[0]).astype(BF16), w_in[:, :width])

    for p in range(pairs):
        lanes = slice(p * pair_width, (p + 1) * pair_width)
        d_o = split(d_att[:, lanes])
        q = split(branch[2, :, lanes] * BF16(0.125))
        k = split(branch[3, :, lanes])
        v = branch[1, :, lanes]
        half = tok // 2
        dv_low = dv_all = dk_low = dk_all = None
        dq = []
        for lo, hi, js in halves:
            dq_sum = None
            for h in range(2):
                d_w = dot_nt(d_o[h][lo:hi], v[:js])
                d_s = (d_w * sslope[2 * p + h, lo:hi, :js]).astype(BF16)
                term = dot(d_s, k[h][:js])
                dq_sum = term if dq_sum is None else dq_sum + term
                dk = dot_tn(d_s, q[h][lo:hi])
                dv = dot_tn(weight[2 * p + h, lo:hi, :js], d_o[h][lo:hi])
                if lo == 0:
                    dk_low = dk if dk_low is None else dk_low + dk
                    dv_low = dv if dv_low is None else dv_low + dv
                else:
                    dk_all = dk if dk_all is None else dk_all + dk
                    dv_all = dv if dv_all is None else dv_all + dv
            dq.append(dq_sum * 0.125)
        dq = jnp.concatenate(dq, axis=0)
        dk = jnp.concatenate([dk_all[:half] + dk_low, dk_all[half:]], axis=0)
        dv = jnp.concatenate([dv_all[:half] + dv_low, dv_all[half:]], axis=0)
        for i, value in ((1, dv), (2, dq), (3, dk)):
            value = value.astype(BF16).astype(F32)
            sides[i - 1, :, lanes] = (value * slope[i, :, lanes]).astype(BF16)

    for i in range(1, 4):
        d_normed = d_normed + dot_nt(sides[i - 1], w_in[:, i * width : (i + 1) * width])
    d_normed = d_normed.astype(BF16).astype(F32)
    d_emb = scale * (
        d_normed
        - jnp.mean(d_normed, axis=-1, keepdims=True)
        - normed * jnp.mean(d_normed * normed, axis=-1, keepdims=True)
    )
    token_grads = (d_emb + cot[...].astype(F32)).astype(BF16)

    spread = dot(place[...], token_grads).astype(BF16)
    for xx in range(nx):
        packed[xx] = spread[:, xx * chunk : (xx + 1) * chunk].reshape(ny, cap, chunk)
    ret[x * ny + y] = packed[x, y]
    for dy, dx in columns:
        yy, xx = in_column(dy, dx)
        send(packed.at[xx, yy], ret.at[x * ny + y], 6, device(yy, z, xx))

    wait_recv(wsw_in, 3)
    wblock = wown.shape[0] // (nz * nx)
    wrs_out[...] = (wown + wsw_in[...].astype(F32)).astype(BF16).reshape(nz * nx, wblock, half_width)
    wrs_in[zx] = wrs_out[zx]
    for dz, dx in planes:
        zz, xx = in_plane(dz, dx)
        send(wrs_out.at[zz * nx + xx], wrs_in.at[zx], 4, device(y, zz, xx))

    wait_recv(idx_all.at[pl.ds(0, (nx - 1) * ny)], 1)
    half_rows = shard_rows // nc
    for s in range(2):
        side = 1 - core if s == 0 else core
        m = iota((half_rows, cap), 0)
        row_at = (m // 16) * 32 + side * 16 + m % 16
        for k in range(nx * ny):
            hot[s, :, k * cap : (k + 1) * cap] = (
                (row_at == idx_all[k][:, :cap]).astype(F32).astype(BF16)
            )

    wait_recv(wrs_in.at[pl.ds(0, nz * nx - 1)], 4)
    wsum = jnp.sum(wrs_in[...].astype(F32), axis=0)
    way_out[...] = wsum.astype(BF16)

    wait_recv(ret.at[pl.ds(0, nx * ny - 1)], 6)
    way_in[y] = way_out[...]
    for dy in near:
        yy, _ = in_column(dy, 0)
        send(way_out, way_in.at[y], 5, device(yy, z, x))
    returned = ret[...].reshape(nx * slots, chunk)
    half_out[...] = dot(hot[0], returned).astype(BF16)
    send(half_out, half_in, 8, sibling)
    own_half = dot(hot[1], returned)
    wait_recv(half_in, 8)
    total = own_half + half_in[...].astype(F32)

    rs_out[...] = total.astype(BF16).reshape(nz * nx, 16, chunk)
    rs_in[zx] = rs_out[zx]
    for dz, dx in planes:
        zz, xx = in_plane(dz, dx)
        send(rs_out.at[zz * nx + xx], rs_in.at[zx], 9, device(y, zz, xx))

    wait_recv(way_in.at[pl.ds(0, ny - 1)], 5)
    wsum = jnp.sum(way_in[...].astype(F32), axis=0)
    wrows = wblock // nc
    wsum = [wsum[c * wrows : (c + 1) * wrows] for c in range(2)]
    wfin_out[...] = jnp.where(core == 0, wsum[1], wsum[0])
    wown = jnp.where(core == 0, wsum[0], wsum[1])
    send(wfin_out, wfin_in, 7, sibling)

    wait_recv(wfin_in, 7)
    wother = wfin_in[...]
    wgrad_ref[:, :half_width] = jnp.where(core == 0, wown, wother).astype(BF16)
    wgrad_ref[:, half_width:] = jnp.where(core == 0, wother, wown).astype(BF16)
    wait_send(idx_own.at[pl.ds(0, ny - 1)], 0)
    wait_send(idx_all.at[pl.ds(0, (nx - 1) * ny)], 1)
    wait_send(fetched.at[pl.ds(0, ny - 1)], 2)
    wait_send(wsw_out, 3)
    wait_send(wrs_out.at[pl.ds(0, nz * nx - 1)], 4)
    wait_send(way_in.at[pl.ds(0, ny - 1)], 5)
    wait_send(ret.at[pl.ds(0, nx * ny - 1)], 6)
    wait_send(wfin_out, 7)
    wait_send(half_out, 8)
    store.wait()
    wait_recv(rs_in.at[pl.ds(0, nz * nx - 1)], 9)
    for xx in range(nx):
        acc = None
        for zz in range(nz):
            term = rs_in[zz * nx + xx].astype(F32)
            acc = term if acc is None else acc + term
        tgrad_ref[:, xx * chunk : (xx + 1) * chunk] = acc
    wait_send(rs_out.at[pl.ds(0, nz * nx - 1)], 9)


def hand_on(*refs):
    for i in range(3):
        refs[3 + i][...] = refs[i][...]


def on_device(ny, nz, nx, cap, table, owner, local_row, lengths, w_in, w_out, cotangent):
    tok, width = cotangent.shape
    shard_rows = table.shape[0]
    chunk = width // nx
    slots = ny * cap
    nc = CORES
    wblock = width // (nz * nx)
    half_width = width // nc
    vmem = pl.BlockSpec(memory_space=pltpu.VMEM)
    anywhere = pl.BlockSpec(memory_space=pl.ANY)
    V = pltpu.VMEM
    scratch = [
        V((1, tok), jnp.int32),
        V((1, tok), jnp.int32),
        V(lengths.shape, jnp.int32),
        V(table.shape, BF16),
        V(w_in.shape, BF16),
        V(w_out.shape, BF16),
        V(cotangent.shape, BF16),
        V(cotangent.shape, BF16),
        V((ny, 1, -(-cap // 128) * 128), jnp.int32),
        V((nx * ny, 1, -(-cap // 128) * 128), jnp.int32),
        V((ny, cap, width), BF16),
        V((ny, cap, width), BF16),
        V((slots, tok), BF16),
        V((2, shard_rows // nc, nx * slots), BF16),
        V((4, tok, width), BF16),
        V((4, tok, width), F32),
        V((HEADS, tok, tok), BF16),
        V((HEADS, tok, tok), F32),
        V((3, tok, width), BF16),
        V((nx, ny, cap, chunk), BF16),
        V((nx * ny, cap, chunk), BF16),
        V((shard_rows // nc, chunk), BF16),
        V((shard_rows // nc, chunk), BF16),
        V((nz * nx, 16, chunk), BF16),
        V((nz * nx, 16, chunk), BF16),
        V((width, half_width), BF16),
        V((width, half_width), BF16),
        V((nz * nx, wblock, half_width), BF16),
        V((nz * nx, wblock, half_width), BF16),
        V((wblock, half_width), BF16),
        V((ny, wblock, half_width), BF16),
        V((wblock // nc, half_width), F32),
        V((wblock // nc, half_width), F32),
        pltpu.SemaphoreType.DMA((7,)),
        pltpu.SemaphoreType.DMA,
        pltpu.SemaphoreType.DMA((10,)),
        pltpu.SemaphoreType.DMA((10,)),
    ]
    results = pl.pallas_call(
        functools.partial(kernel, ny, nz, nx, cap),
        out_shape=(
            jax.ShapeDtypeStruct((tok, width), BF16),
            jax.ShapeDtypeStruct((shard_rows // (nz * nx * nc), width), F32),
            jax.ShapeDtypeStruct((wblock // nc, width), BF16),
        ),
        in_specs=[anywhere] * 7,
        out_specs=(anywhere, vmem, vmem),
        scratch_shapes=scratch,
        compiler_params=pltpu.CompilerParams(
            collective_id=0, has_side_effects=True, vmem_limit_bytes=56 * 1024 * 1024
        ),
        name="hstu",
    )(
        owner.reshape(1, tok),
        local_row.reshape(1, tok),
        lengths,
        table,
        w_in,
        w_out,
        cotangent,
    )
    return pl.pallas_call(
        hand_on,
        out_shape=tuple(jax.ShapeDtypeStruct(r.shape, r.dtype) for r in results),
        in_specs=[vmem] * 3,
        out_specs=(vmem,) * 3,
        name="hand_on",
    )(*results)


def build(mesh, nx, cap):
    ny = mesh.shape["table"]
    nz = mesh.shape["batch"] // (nx * CORES)
    return jax.shard_map(
        functools.partial(on_device, ny, nz, nx, cap),
        mesh=mesh,
        in_specs=(
            P("table", None),
            P(("table", "batch"), None),
            P(("table", "batch")),
            P(("table", "batch"), None),
            P(),
            P(),
            P(("table", "batch"), None),
        ),
        out_specs=(P(("table", "batch"), None), P(("table", "batch"), None), P("batch", None)),
        check_vma=False,
    )


def solution(mesh):
    return build(mesh, 4, 48)
```

```python
import functools

import jax
import jax.numpy as jnp
from jax import lax
from jax.experimental import pallas as pl
from jax.experimental.pallas import tpu as pltpu
from jax.sharding import PartitionSpec as P

HEADS = 8
MOST_LEN = 192
EPSILON = 1e-05
CORES = 2
F32 = jnp.float32
BF16 = jnp.bfloat16


def dot(a, b):
    return lax.dot_general(a, b, (((1,), (0,)), ((), ())), preferred_element_type=F32)


def dot_nt(a, b):
    return lax.dot_general(a, b, (((1,), (1,)), ((), ())), preferred_element_type=F32)


def dot_tn(a, b):
    return lax.dot_general(a, b, (((0,), (0,)), ((), ())), preferred_element_type=F32)


def iota(shape, dim):
    return lax.broadcasted_iota(jnp.int32, shape, dim)


def sigmoid(z):
    return 0.5 * jnp.tanh(0.5 * z) + 0.5


def far_first(n):
    return sorted(range(n), key=lambda d: -min(d, n - d))


def kernel(
    ny, nz, nx, cap,
    owner_hbm, row_hbm, len_hbm, table_hbm, w_in_hbm, w_out_hbm, cot_hbm,
    out_hbm, tgrad_ref, wgrad_ref,
    owner_ref, row_ref, len_ref, table, w_in, w_out, cot, out,
    idx_own, idx_all, reply, fetched, place, hot,
    branch, slope, weight, sslope, sides,
    packed, ret, half_out, half_in, rs_out, rs_in,
    wsw_out, wsw_in, wrs_out, wrs_in, way_out, way_in, wfin_out, wfin_in,
    load_sem, store_sem, send_sem, recv_sem,
):
    tok, width = cot.shape
    nc = CORES
    pair_width = 128
    pairs = width // pair_width
    chunk = width // nx
    half_width = width // nc
    slots = ny * cap
    listed_width = idx_own.shape[-1]
    y = lax.axis_index("table")
    b = lax.axis_index("batch")
    core = b % nc
    x = (b // nc) % nx
    z = b // (nc * nx)
    zx = z * nx + x
    sibling = {"table": y, "batch": zx * nc + (1 - core)}

    def device(yy, zz, xx):
        return {"table": yy, "batch": (zz * nx + xx) * nc + core}

    columns = [(dy, dx) for dy in far_first(ny) for dx in far_first(nx) if (dy, dx) != (0, 0)]
    planes = [(dz, dx) for dz in far_first(nz) for dx in far_first(nx) if (dz, dx) != (0, 0)]

    own_column, own_plane = len(columns), len(planes)

    def in_column(dy, dx):
        return (y + dy) & (ny - 1), (x + dx) & (nx - 1)

    def in_plane(dz, dx):
        return (z + dz) & (nz - 1), (x + dx) & (nx - 1)

    barrier = pltpu.get_barrier_semaphore()
    greeted = 0
    axes = (
        [device((y + d) & (ny - 1), z, x) for d in far_first(ny) if d]
        + [device(y, (z + d) & (nz - 1), x) for d in far_first(nz) if d]
        + [device(y, z, (x + d) & (nx - 1)) for d in far_first(nx) if d]
    )
    for target in axes:
        pl.semaphore_signal(barrier, inc=1, device_id=target)
        greeted += 1
    pl.semaphore_signal(barrier, inc=1, device_id=sibling)
    greeted += 1

    loads = [
        pltpu.make_async_copy(src, dst, load_sem.at[i])
        for i, (src, dst) in enumerate(
            [
                (owner_hbm, owner_ref),
                (row_hbm, row_ref),
                (table_hbm, table),
                (len_hbm, len_ref),
                (cot_hbm, cot),
                (w_out_hbm, w_out),
                (w_in_hbm, w_in),
            ]
        )
    ]
    for load in loads:
        load.start()

    loads[0].wait()
    loads[1].wait()
    owner = owner_ref[...]
    rows = row_ref[...]
    mine = (iota((ny, tok), 0) == owner).astype(F32)
    earlier = (iota((tok, tok), 0) < iota((tok, tok), 1)).astype(F32).astype(BF16)
    before = dot(mine.astype(BF16), earlier)
    rank = jnp.sum(mine * before, axis=0, keepdims=True).astype(jnp.int32)
    rank_hot = (iota((listed_width, tok), 0) == rank).astype(F32).astype(BF16)
    high = (rows // 32).astype(F32)
    low = (rows % 32).astype(F32)
    parts = jnp.concatenate([mine * high, mine * low], axis=0).astype(BF16)
    listed = dot_nt(parts, rank_hot)
    listed = (listed[:ny] * 32.0 + listed[ny:]).astype(jnp.int32)
    for o in range(ny):
        idx_own[o] = listed[o : o + 1]
    idx_all[own_column] = idx_own[y]
    slot = owner * cap + rank
    place[...] = (iota((slots, tok), 0) == slot).astype(F32).astype(BF16)
    slot_col = jnp.broadcast_to(slot.astype(F32), (8, tok)).T[:, :1].astype(jnp.int32)
    unplace = (iota((tok, slots), 1) == slot_col).astype(F32).astype(BF16)

    pl.semaphore_wait(barrier, greeted)

    def send(src, dst, stage, target):
        copy = pltpu.make_async_remote_copy(
            src_ref=src,
            dst_ref=dst,
            send_sem=send_sem.at[stage],
            recv_sem=recv_sem.at[stage],
            device_id=target,
        )
        copy.start()

    def wait_recv(slab, stage):
        pltpu.make_async_copy(slab, slab, recv_sem.at[stage]).wait()

    def wait_send(slab, stage):
        pltpu.make_async_copy(slab, slab, send_sem.at[stage]).wait()

    near = [dy for dy in far_first(ny) if dy]
    for dy in near:
        yy, _ = in_column(dy, 0)
        send(idx_own.at[yy], idx_all.at[columns.index((dy, 0))], 0, device(yy, z, x))
    loads[2].wait()
    wait_recv(idx_all.at[pl.ds(0, ny - 1)], 0)

    order = far_first(ny)
    asked = [idx_all[columns.index((dy, 0)) if dy else own_column] for dy in order]
    if ny < 8:
        asked = asked + [asked[0]] * (8 - ny)
    asked = jnp.concatenate(asked, axis=0).astype(F32).T.astype(jnp.int32)
    shard_rows = table.shape[0]
    group = 2
    for g in range(0, ny, group):
        picks = jnp.concatenate(
            [iota((cap, shard_rows), 1) == asked[:cap, k : k + 1] for k in range(g, g + group)], axis=0
        )
        found = dot(picks.astype(F32).astype(BF16), table[...]).astype(BF16)
        for k in range(g, g + group):
            dy = order[k]
            block = found[(k - g) * cap : (k - g + 1) * cap]
            if dy == 0:
                fetched[y] = block
            else:
                reply[k] = block
                yy, _ = in_column(-dy, 0)
                send(reply.at[k], fetched.at[y], 2, device(yy, z, x))

    for j, (dy, dx) in enumerate(columns):
        if dx:
            yy, xx = in_column(dy, dx)
            send(idx_own.at[yy], idx_all.at[j], 1, device(yy, z, xx))

    loads[3].wait()
    loads[4].wait()
    loads[5].wait()
    dg = dot_nt(cot[...], w_out[...]).astype(BF16).astype(F32)
    bound = len_ref[:, :1]
    place_i = iota((tok, tok), 0)
    place_j = iota((tok, tok), 1)
    allowed = ((place_i >= bound) == (place_j >= bound)) & (place_j <= place_i)
    mask = jnp.where(allowed, 1.0 / MOST_LEN, 0.0).astype(F32)
    loads[6].wait()

    wait_recv(fetched.at[pl.ds(0, ny - 1)], 2)

    embedded = dot(unplace, fetched[...].reshape(slots, width)).astype(BF16)
    embedded = embedded.astype(F32)
    center = jnp.mean(embedded, axis=-1, keepdims=True)
    shifted = embedded - center
    scale = lax.rsqrt(jnp.mean(shifted * shifted, axis=-1, keepdims=True) + EPSILON)
    normed = shifted * scale
    normed_b = normed.astype(BF16)
    for i in range(4):
        hidden = dot(normed_b, w_in[:, i * width : (i + 1) * width])
        sig = sigmoid(hidden)
        value = hidden * sig
        branch[i] = value.astype(BF16)
        slope[i] = sig + value * (1.0 - sig)

    first_lane = iota((tok, pair_width), 1) < width // HEADS
    halves = [(0, tok // 2, tok // 2), (tok // 2, tok, tok)]

    def split(values):
        zero = jnp.zeros_like(values)
        return jnp.where(first_lane, values, zero), jnp.where(first_lane, zero, values)

    attended = []
    for p in range(pairs):
        lanes = slice(p * pair_width, (p + 1) * pair_width)
        v = split(branch[1, :, lanes])
        q = split(branch[2, :, lanes] * BF16(0.125))
        k = branch[3, :, lanes]
        result = []
        for lo, hi, js in halves:
            total = None
            for h in range(2):
                score = dot_nt(q[h][lo:hi], k[:js])
                sig = sigmoid(score)
                value = score * sig
                m = mask[lo:hi, :js]
                w = (value * m).astype(BF16)
                weight[2 * p + h, lo:hi, :js] = w
                sslope[2 * p + h, lo:hi, :js] = (sig + value * (1.0 - sig)) * m
                term = dot(w, v[h][:js])
                total = term if total is None else total + term
            result.append(total)
        attended.append(jnp.concatenate(result, axis=0))
    attended = jnp.concatenate(attended, axis=1)
    center2 = jnp.mean(attended, axis=-1, keepdims=True)
    shifted2 = attended - center2
    scale2 = lax.rsqrt(jnp.mean(shifted2 * shifted2, axis=-1, keepdims=True) + EPSILON)
    normed2 = shifted2 * scale2
    gate = branch[0].astype(F32)
    gated = (normed2 * gate).astype(BF16)

    wgrad = dot_tn(gated, cot[...])
    wgrad = [wgrad[:, c * half_width : (c + 1) * half_width] for c in range(2)]
    wsw_out[...] = jnp.where(core == 0, wgrad[1], wgrad[0]).astype(BF16)
    wown = jnp.where(core == 0, wgrad[0], wgrad[1])
    send(wsw_out, wsw_in, 3, sibling)

    out[...] = (dot(gated, w_out[...]) + embedded).astype(BF16)
    store = pltpu.make_async_copy(out, out_hbm, store_sem)
    store.start()

    d_n2 = dg * gate
    d_gate = (dg * normed2).astype(BF16).astype(F32)
    d_att = scale2 * (
        d_n2
        - jnp.mean(d_n2, axis=-1, keepdims=True)
        - normed2 * jnp.mean(d_n2 * normed2, axis=-1, keepdims=True)
    )
    d_att = d_att.astype(BF16)
    d_normed = dot_nt((d_gate * slope[0]).astype(BF16), w_in[:, :width])

    for p in range(pairs):
        lanes = slice(p * pair_width, (p + 1) * pair_width)
        d_o = split(d_att[:, lanes])
        q = split(branch[2, :, lanes] * BF16(0.125))
        k = split(branch[3, :, lanes])
        v = branch[1, :, lanes]
        half = tok // 2
        dv_low = dv_all = dk_low = dk_all = None
        dq = []
        for lo, hi, js in halves:
            dq_sum = None
            for h in range(2):
                d_w = dot_nt(d_o[h][lo:hi], v[:js])
                d_s = (d_w * sslope[2 * p + h, lo:hi, :js]).astype(BF16)
                term = dot(d_s, k[h][:js])
                dq_sum = term if dq_sum is None else dq_sum + term
                dk = dot_tn(d_s, q[h][lo:hi])
                dv = dot_tn(weight[2 * p + h, lo:hi, :js], d_o[h][lo:hi])
                if lo == 0:
                    dk_low = dk if dk_low is None else dk_low + dk
                    dv_low = dv if dv_low is None else dv_low + dv
                else:
                    dk_all = dk if dk_all is None else dk_all + dk
                    dv_all = dv if dv_all is None else dv_all + dv
            dq.append(dq_sum * 0.125)
        dq = jnp.concatenate(dq, axis=0)
        dk = jnp.concatenate([dk_all[:half] + dk_low, dk_all[half:]], axis=0)
        dv = jnp.concatenate([dv_all[:half] + dv_low, dv_all[half:]], axis=0)
        for i, value in ((1, dv), (2, dq), (3, dk)):
            value = value.astype(BF16).astype(F32)
            sides[i - 1, :, lanes] = (value * slope[i, :, lanes]).astype(BF16)

    for i in range(1, 4):
        d_normed = d_normed + dot_nt(sides[i - 1], w_in[:, i * width : (i + 1) * width])
    d_normed = d_normed.astype(BF16).astype(F32)
    d_emb = scale * (
        d_normed
        - jnp.mean(d_normed, axis=-1, keepdims=True)
        - normed * jnp.mean(d_normed * normed, axis=-1, keepdims=True)
    )
    token_grads = (d_emb + cot[...].astype(F32)).astype(BF16)

    parts_of = 4 if nx * ny >= 8 else 2
    part = nx * ny // parts_of
    last = parts_of - 1
    arrivals = 10
    spread = dot(place[...], token_grads).astype(BF16)
    for xx in range(nx):
        packed[xx] = spread[:, xx * chunk : (xx + 1) * chunk].reshape(ny, cap, chunk)
    ret[own_column] = packed[x, y]
    for j, (dy, dx) in enumerate(columns):
        yy, xx = in_column(dy, dx)
        send(packed.at[xx, yy], ret.at[j], arrivals + j // part, device(yy, z, xx))

    wait_recv(idx_all.at[pl.ds(0, (nx - 1) * ny)], 1)
    wait_recv(wsw_in, 3)
    wblock = wown.shape[0] // (nz * nx)
    wrs_out[...] = (wown + wsw_in[...].astype(F32)).astype(BF16).reshape(nz * nx, wblock, half_width)
    wrs_in[zx] = wrs_out[zx]
    for dz, dx in planes:
        zz, xx = in_plane(dz, dx)
        send(wrs_out.at[zz * nx + xx], wrs_in.at[zx], 4, device(y, zz, xx))

    half_rows = shard_rows // nc
    m = iota((16, nx * slots), 0)
    starts = [(z_ * nx + x_) * 32 for z_, x_ in [in_plane(*d) for d in planes + [(0, 0)]]]
    listed = jnp.concatenate([idx_all[j][:, :cap] for j in range(nx * ny)], axis=1)
    for s in range(2):
        side = 1 - core if s == 0 else core
        for g, start in enumerate(starts):
            hot[s, g * 16 : (g + 1) * 16] = (
                (m + (start + side * 16) == listed).astype(F32).astype(BF16)
            )

    sums = [None, None]
    for a in range(last):
        wait_recv(ret.at[pl.ds(0, part)], arrivals + a)
        block = ret[a * part : (a + 1) * part].reshape(part * cap, chunk)
        for s in range(2):
            term = dot(hot[s, :, a * part * cap : (a + 1) * part * cap], block)
            sums[s] = term if a == 0 else sums[s] + term

    wait_recv(wrs_in.at[pl.ds(0, nz * nx - 1)], 4)
    wsum = jnp.sum(wrs_in[...].astype(F32), axis=0)
    way_out[...] = wsum.astype(BF16)

    wait_recv(ret.at[pl.ds(0, part - 1)], arrivals + last)
    block = ret[last * part :].reshape(part * cap, chunk)
    pieces = [slice(0, half_rows // 2), slice(half_rows // 2, half_rows)]

    def piece_sum(s, piece):
        return sums[s][piece] + dot(hot[s, piece, last * part * cap :], block)

    for stage, piece in zip((6, 8), pieces):
        half_out[piece] = piece_sum(0, piece).astype(BF16)
        send(half_out.at[piece], half_in.at[piece], stage, sibling)
    way_in[y] = way_out[...]
    for dy in near:
        yy, _ = in_column(dy, 0)
        send(way_out, way_in.at[y], 5, device(yy, z, x))
    own = [piece_sum(1, piece) for piece in pieces]

    groups = nz * nx // 2
    for i, (stage, piece) in enumerate(zip((6, 8), pieces)):
        wait_recv(half_in.at[piece], stage)
        total = own[i] + half_in[piece].astype(F32)
        rs_out[i * groups : (i + 1) * groups] = total.astype(BF16).reshape(groups, 16, chunk)
        for g in range(i * groups, min((i + 1) * groups, own_plane)):
            zz, xx = in_plane(*planes[g])
            send(rs_out.at[g], rs_in.at[g], 9, device(y, zz, xx))
    rs_in[own_plane] = rs_out[own_plane]

    wait_recv(way_in.at[pl.ds(0, ny - 1)], 5)
    wsum = jnp.sum(way_in[...].astype(F32), axis=0)
    wrows = wblock // nc
    wsum = [wsum[c * wrows : (c + 1) * wrows] for c in range(2)]
    wfin_out[...] = jnp.where(core == 0, wsum[1], wsum[0])
    wown = jnp.where(core == 0, wsum[0], wsum[1])
    send(wfin_out, wfin_in, 7, sibling)

    wait_recv(wfin_in, 7)
    wother = wfin_in[...]
    wgrad_ref[:, :half_width] = jnp.where(core == 0, wown, wother).astype(BF16)
    wgrad_ref[:, half_width:] = jnp.where(core == 0, wother, wown).astype(BF16)
    wait_send(idx_own.at[pl.ds(0, ny - 1)], 0)
    wait_send(idx_all.at[pl.ds(0, (nx - 1) * ny)], 1)
    wait_send(fetched.at[pl.ds(0, ny - 1)], 2)
    wait_send(wsw_out, 3)
    wait_send(wrs_out.at[pl.ds(0, nz * nx - 1)], 4)
    wait_send(way_in.at[pl.ds(0, ny - 1)], 5)
    for a in range(parts_of):
        wait_send(ret.at[pl.ds(0, part - (a == last))], arrivals + a)
    wait_send(wfin_out, 7)
    for stage, piece in zip((6, 8), pieces):
        wait_send(half_out.at[piece], stage)
    store.wait()
    wait_recv(rs_in.at[pl.ds(0, nz * nx - 1)], 9)
    for dx in range(nx):
        acc = None
        for g, (dz, dx_) in enumerate(planes + [(0, 0)]):
            if dx_ == dx:
                term = rs_in[g].astype(F32)
                acc = term if acc is None else acc + term
        start = pl.multiple_of(((x - dx) & (nx - 1)) * chunk, chunk)
        tgrad_ref[:, pl.ds(start, chunk)] = acc
    wait_send(rs_out.at[pl.ds(0, nz * nx - 1)], 9)


def hand_on(*refs):
    given, results, held = refs[:3], refs[3:6], refs[6:9]
    in_sem, out_sem = refs[9:]
    ins = [pltpu.make_async_copy(given[i], held[i], in_sem.at[i]) for i in range(3)]
    outs = [pltpu.make_async_copy(held[i], results[i], out_sem.at[i]) for i in range(3)]
    for copy in ins:
        copy.start()
    for i in range(3):
        ins[i].wait()
        outs[i].start()
    for copy in outs:
        copy.wait()


def on_device(ny, nz, nx, cap, table, owner, local_row, lengths, w_in, w_out, cotangent):
    tok, width = cotangent.shape
    shard_rows = table.shape[0]
    chunk = width // nx
    slots = ny * cap
    nc = CORES
    wblock = width // (nz * nx)
    half_width = width // nc
    vmem = pl.BlockSpec(memory_space=pltpu.VMEM)
    anywhere = pl.BlockSpec(memory_space=pl.ANY)
    V = pltpu.VMEM
    scratch = [
        V((1, tok), jnp.int32),
        V((1, tok), jnp.int32),
        V(lengths.shape, jnp.int32),
        V(table.shape, BF16),
        V(w_in.shape, BF16),
        V(w_out.shape, BF16),
        V(cotangent.shape, BF16),
        V(cotangent.shape, BF16),
        V((ny, 1, -(-cap // 128) * 128), jnp.int32),
        V((nx * ny, 1, -(-cap // 128) * 128), jnp.int32),
        V((ny, cap, width), BF16),
        V((ny, cap, width), BF16),
        V((slots, tok), BF16),
        V((2, shard_rows // nc, nx * slots), BF16),
        V((4, tok, width), BF16),
        V((4, tok, width), F32),
        V((HEADS, tok, tok), BF16),
        V((HEADS, tok, tok), F32),
        V((3, tok, width), BF16),
        V((nx, ny, cap, chunk), BF16),
        V((nx * ny, cap, chunk), BF16),
        V((shard_rows // nc, chunk), BF16),
        V((shard_rows // nc, chunk), BF16),
        V((nz * nx, 16, chunk), BF16),
        V((nz * nx, 16, chunk), BF16),
        V((width, half_width), BF16),
        V((width, half_width), BF16),
        V((nz * nx, wblock, half_width), BF16),
        V((nz * nx, wblock, half_width), BF16),
        V((wblock, half_width), BF16),
        V((ny, wblock, half_width), BF16),
        V((wblock // nc, half_width), F32),
        V((wblock // nc, half_width), F32),
        pltpu.SemaphoreType.DMA((7,)),
        pltpu.SemaphoreType.DMA,
        pltpu.SemaphoreType.DMA((14,)),
        pltpu.SemaphoreType.DMA((14,)),
    ]
    results = pl.pallas_call(
        functools.partial(kernel, ny, nz, nx, cap),
        out_shape=(
            jax.ShapeDtypeStruct((tok, width), BF16),
            jax.ShapeDtypeStruct((shard_rows // (nz * nx * nc), width), F32),
            jax.ShapeDtypeStruct((wblock // nc, width), BF16),
        ),
        in_specs=[anywhere] * 7,
        out_specs=(anywhere, vmem, vmem),
        scratch_shapes=scratch,
        compiler_params=pltpu.CompilerParams(
            collective_id=0, has_side_effects=True, fuse_transposed_lhs_in_matmul=True, vmem_limit_bytes=56 * 1024 * 1024
        ),
        name="hstu",
    )(
        owner.reshape(1, tok),
        local_row.reshape(1, tok),
        lengths,
        table,
        w_in,
        w_out,
        cotangent,
    )
    return pl.pallas_call(
        hand_on,
        out_shape=tuple(jax.ShapeDtypeStruct(r.shape, r.dtype) for r in results),
        in_specs=[anywhere] * 3,
        out_specs=(anywhere,) * 3,
        scratch_shapes=[V(r.shape, r.dtype) for r in results]
        + [pltpu.SemaphoreType.DMA((3,)), pltpu.SemaphoreType.DMA((3,))],
        name="hand_on",
    )(*results)


def build(mesh, nx, cap):
    ny = mesh.shape["table"]
    nz = mesh.shape["batch"] // (nx * CORES)
    return jax.shard_map(
        functools.partial(on_device, ny, nz, nx, cap),
        mesh=mesh,
        in_specs=(
            P("table", None),
            P(("table", "batch"), None),
            P(("table", "batch")),
            P(("table", "batch"), None),
            P(),
            P(),
            P(("table", "batch"), None),
        ),
        out_specs=(P(("table", "batch"), None), P(("table", "batch"), None), P("batch", None)),
        check_vma=False,
    )


def solution(mesh):
    return build(mesh, 4, 48)
```

```python
import functools

import jax
import jax.numpy as jnp
from jax import lax
from jax.experimental import pallas as pl
from jax.experimental.pallas import tpu as pltpu
from jax.sharding import PartitionSpec as P

HEADS = 8
MOST_LEN = 192
EPSILON = 1e-05
CORES = 2
F32 = jnp.float32
BF16 = jnp.bfloat16


def dot(a, b):
    return lax.dot_general(a, b, (((1,), (0,)), ((), ())), preferred_element_type=F32)


def dot_nt(a, b):
    return lax.dot_general(a, b, (((1,), (1,)), ((), ())), preferred_element_type=F32)


def dot_tn(a, b):
    return lax.dot_general(a, b, (((0,), (0,)), ((), ())), preferred_element_type=F32)


def iota(shape, dim):
    return lax.broadcasted_iota(jnp.int32, shape, dim)


def sigmoid(z):
    return 0.5 * jnp.tanh(0.5 * z) + 0.5


def far_first(n):
    return sorted(range(n), key=lambda d: -min(d, n - d))


def kernel(
    ny, nz, nx, cap,
    owner_hbm, row_hbm, len_hbm, table_hbm, w_in_hbm, w_out_hbm, cot_hbm,
    out_hbm, tgrad_ref, wgrad_ref,
    owner_ref, row_ref, len_ref, table, w_in, w_out, cot, out,
    idx_own, idx_all, reply, fetched, place, hot,
    branch, slope, weight, sslope, sides,
    packed, ret, half_out, half_in, rs_out, rs_in,
    wsw_out, wsw_in, wrs_out, wrs_in, way_out, way_in, wfin_out, wfin_in,
    load_sem, store_sem, send_sem, recv_sem,
):
    tok, width = cot.shape
    nc = CORES
    pair_width = 128
    pairs = width // pair_width
    chunk = width // nx
    half_width = width // nc
    slots = ny * cap
    listed_width = idx_own.shape[-1]
    y = lax.axis_index("table")
    b = lax.axis_index("batch")
    core = b % nc
    x = (b // nc) % nx
    z = b // (nc * nx)
    zx = z * nx + x
    sibling = {"table": y, "batch": zx * nc + (1 - core)}

    def device(yy, zz, xx):
        return {"table": yy, "batch": (zz * nx + xx) * nc + core}

    columns = [(dy, dx) for dy in far_first(ny) for dx in far_first(nx) if (dy, dx) != (0, 0)]
    planes = [(dz, dx) for dz in far_first(nz) for dx in far_first(nx) if (dz, dx) != (0, 0)]

    own_column, own_plane = len(columns), len(planes)

    def in_column(dy, dx):
        return (y + dy) & (ny - 1), (x + dx) & (nx - 1)

    def in_plane(dz, dx):
        return (z + dz) & (nz - 1), (x + dx) & (nx - 1)

    barrier = pltpu.get_barrier_semaphore()
    greeted = 0
    axes = (
        [device((y + d) & (ny - 1), z, x) for d in far_first(ny) if d]
        + [device(y, (z + d) & (nz - 1), x) for d in far_first(nz) if d]
        + [device(y, z, (x + d) & (nx - 1)) for d in far_first(nx) if d]
    )
    for target in axes:
        pl.semaphore_signal(barrier, inc=1, device_id=target)
        greeted += 1
    pl.semaphore_signal(barrier, inc=1, device_id=sibling)
    greeted += 1

    loads = [
        pltpu.make_async_copy(src, dst, load_sem.at[i])
        for i, (src, dst) in enumerate(
            [
                (owner_hbm, owner_ref),
                (row_hbm, row_ref),
                (table_hbm, table),
                (len_hbm, len_ref),
                (cot_hbm, cot),
                (w_out_hbm, w_out),
                (w_in_hbm, w_in),
            ]
        )
    ]
    for load in loads:
        load.start()

    loads[0].wait()
    loads[1].wait()
    owner = owner_ref[...]
    rows = row_ref[...]
    mine = (iota((ny, tok), 0) == owner).astype(F32)
    earlier = (iota((tok, tok), 0) < iota((tok, tok), 1)).astype(F32).astype(BF16)
    before = dot(mine.astype(BF16), earlier)
    rank = jnp.sum(mine * before, axis=0, keepdims=True).astype(jnp.int32)
    rank_hot = (iota((listed_width, tok), 0) == rank).astype(F32).astype(BF16)
    high = (rows // 32).astype(F32)
    low = (rows % 32).astype(F32)
    parts = jnp.concatenate([mine * high, mine * low], axis=0).astype(BF16)
    listed = dot_nt(parts, rank_hot)
    listed = (listed[:ny] * 32.0 + listed[ny:]).astype(jnp.int32)
    for o in range(ny):
        idx_own[o] = listed[o : o + 1]
    idx_all[own_column] = idx_own[y]
    slot = owner * cap + rank
    place[...] = (iota((slots, tok), 0) == slot).astype(F32).astype(BF16)
    slot_col = jnp.broadcast_to(slot.astype(F32), (8, tok)).T[:, :1].astype(jnp.int32)
    unplace = (iota((tok, slots), 1) == slot_col).astype(F32).astype(BF16)

    pl.semaphore_wait(barrier, greeted)

    def send(src, dst, stage, target):
        copy = pltpu.make_async_remote_copy(
            src_ref=src,
            dst_ref=dst,
            send_sem=send_sem.at[stage],
            recv_sem=recv_sem.at[stage],
            device_id=target,
        )
        copy.start()

    def wait_recv(slab, stage):
        pltpu.make_async_copy(slab, slab, recv_sem.at[stage]).wait()

    def wait_send(slab, stage):
        pltpu.make_async_copy(slab, slab, send_sem.at[stage]).wait()

    near = [dy for dy in far_first(ny) if dy]
    lists = 13
    for dy in near:
        yy, _ = in_column(dy, 0)
        send(idx_own.at[yy], idx_all.at[columns.index((dy, 0))], lists + dy, device(yy, z, x))
    loads[2].wait()

    order = near[::-1] + [0]
    shard_rows = table.shape[0]
    group = 2
    for first in range(0, ny, group):
        turn = order[first : first + group]
        for dy in turn:
            if dy:
                wait_recv(idx_all.at[pl.ds(0, 1)], lists + dy)
        asked = [idx_all[columns.index((dy, 0)) if dy else own_column] for dy in turn]
        asked = jnp.concatenate(asked * (8 // group), axis=0).astype(F32).T.astype(jnp.int32)
        picks = jnp.concatenate(
            [iota((cap, shard_rows), 1) == asked[:cap, k : k + 1] for k in range(group)], axis=0
        )
        found = dot(picks.astype(F32).astype(BF16), table[...]).astype(BF16)
        for k, dy in enumerate(turn):
            block = found[k * cap : (k + 1) * cap]
            if dy == 0:
                fetched[y] = block
            else:
                reply[dy] = block
                yy, _ = in_column(-dy, 0)
                send(reply.at[dy], fetched.at[y], 2, device(yy, z, x))

    for j, (dy, dx) in enumerate(columns):
        if dx:
            yy, xx = in_column(dy, dx)
            send(idx_own.at[yy], idx_all.at[j], 1, device(yy, z, xx))

    loads[3].wait()
    loads[4].wait()
    loads[5].wait()
    dg = dot_nt(cot[...], w_out[...]).astype(BF16).astype(F32)
    bound = len_ref[:, :1]
    place_i = iota((tok, tok), 0)
    place_j = iota((tok, tok), 1)
    allowed = ((place_i >= bound) == (place_j >= bound)) & (place_j <= place_i)
    mask = jnp.where(allowed, 1.0 / MOST_LEN, 0.0).astype(F32)
    loads[6].wait()

    wait_recv(fetched.at[pl.ds(0, ny - 1)], 2)

    embedded = dot(unplace, fetched[...].reshape(slots, width)).astype(BF16)
    embedded = embedded.astype(F32)
    center = jnp.mean(embedded, axis=-1, keepdims=True)
    shifted = embedded - center
    scale = lax.rsqrt(jnp.mean(shifted * shifted, axis=-1, keepdims=True) + EPSILON)
    normed = shifted * scale
    normed_b = normed.astype(BF16)
    for i in range(4):
        hidden = dot(normed_b, w_in[:, i * width : (i + 1) * width])
        sig = sigmoid(hidden)
        value = hidden * sig
        branch[i] = value.astype(BF16)
        slope[i] = sig + value * (1.0 - sig)

    first_lane = iota((tok, pair_width), 1) < width // HEADS
    halves = [(0, tok // 2, tok // 2), (tok // 2, tok, tok)]

    def split(values):
        zero = jnp.zeros_like(values)
        return jnp.where(first_lane, values, zero), jnp.where(first_lane, zero, values)

    attended = []
    for p in range(pairs):
        lanes = slice(p * pair_width, (p + 1) * pair_width)
        v = split(branch[1, :, lanes])
        q = split(branch[2, :, lanes] * BF16(0.125))
        k = branch[3, :, lanes]
        result = []
        for lo, hi, js in halves:
            total = None
            for h in range(2):
                score = dot_nt(q[h][lo:hi], k[:js])
                sig = sigmoid(score)
                value = score * sig
                m = mask[lo:hi, :js]
                w = (value * m).astype(BF16)
                weight[2 * p + h, lo:hi, :js] = w
                sslope[2 * p + h, lo:hi, :js] = (sig + value * (1.0 - sig)) * m
                term = dot(w, v[h][:js])
                total = term if total is None else total + term
            result.append(total)
        attended.append(jnp.concatenate(result, axis=0))
    attended = jnp.concatenate(attended, axis=1)
    center2 = jnp.mean(attended, axis=-1, keepdims=True)
    shifted2 = attended - center2
    scale2 = lax.rsqrt(jnp.mean(shifted2 * shifted2, axis=-1, keepdims=True) + EPSILON)
    normed2 = shifted2 * scale2
    gate = branch[0].astype(F32)
    gated = (normed2 * gate).astype(BF16)

    wgrad = dot_tn(gated, cot[...])
    wgrad = [wgrad[:, c * half_width : (c + 1) * half_width] for c in range(2)]
    wsw_out[...] = jnp.where(core == 0, wgrad[1], wgrad[0]).astype(BF16)
    wown = jnp.where(core == 0, wgrad[0], wgrad[1])
    send(wsw_out, wsw_in, 3, sibling)

    out[...] = (dot(gated, w_out[...]) + embedded).astype(BF16)
    store = pltpu.make_async_copy(out, out_hbm, store_sem)
    store.start()

    d_n2 = dg * gate
    d_gate = (dg * normed2).astype(BF16).astype(F32)
    d_att = scale2 * (
        d_n2
        - jnp.mean(d_n2, axis=-1, keepdims=True)
        - normed2 * jnp.mean(d_n2 * normed2, axis=-1, keepdims=True)
    )
    d_att = d_att.astype(BF16)
    d_normed = dot_nt((d_gate * slope[0]).astype(BF16), w_in[:, :width])

    for p in range(pairs):
        lanes = slice(p * pair_width, (p + 1) * pair_width)
        d_o = split(d_att[:, lanes])
        q = split(branch[2, :, lanes] * BF16(0.125))
        k = split(branch[3, :, lanes])
        v = branch[1, :, lanes]
        half = tok // 2
        dv_low = dv_all = dk_low = dk_all = None
        dq = []
        for lo, hi, js in halves:
            dq_sum = None
            for h in range(2):
                d_w = dot_nt(d_o[h][lo:hi], v[:js])
                d_s = (d_w * sslope[2 * p + h, lo:hi, :js]).astype(BF16)
                term = dot(d_s, k[h][:js])
                dq_sum = term if dq_sum is None else dq_sum + term
                dk = dot_tn(d_s, q[h][lo:hi])
                dv = dot_tn(weight[2 * p + h, lo:hi, :js], d_o[h][lo:hi])
                if lo == 0:
                    dk_low = dk if dk_low is None else dk_low + dk
                    dv_low = dv if dv_low is None else dv_low + dv
                else:
                    dk_all = dk if dk_all is None else dk_all + dk
                    dv_all = dv if dv_all is None else dv_all + dv
            dq.append(dq_sum * 0.125)
        dq = jnp.concatenate(dq, axis=0)
        dk = jnp.concatenate([dk_all[:half] + dk_low, dk_all[half:]], axis=0)
        dv = jnp.concatenate([dv_all[:half] + dv_low, dv_all[half:]], axis=0)
        for i, value in ((1, dv), (2, dq), (3, dk)):
            value = value.astype(BF16).astype(F32)
            sides[i - 1, :, lanes] = (value * slope[i, :, lanes]).astype(BF16)

    for i in range(1, 4):
        d_normed = d_normed + dot_nt(sides[i - 1], w_in[:, i * width : (i + 1) * width])
    d_normed = d_normed.astype(BF16).astype(F32)
    d_emb = scale * (
        d_normed
        - jnp.mean(d_normed, axis=-1, keepdims=True)
        - normed * jnp.mean(d_normed * normed, axis=-1, keepdims=True)
    )
    token_grads = (d_emb + cot[...].astype(F32)).astype(BF16)

    parts_of = 4 if nx * ny >= 8 else 2
    part = nx * ny // parts_of
    last = parts_of - 1
    arrivals = 10
    spread = dot(place[...], token_grads).astype(BF16)
    for xx in range(nx):
        packed[xx] = spread[:, xx * chunk : (xx + 1) * chunk].reshape(ny, cap, chunk)
    ret[own_column] = packed[x, y]
    for j, (dy, dx) in enumerate(columns):
        yy, xx = in_column(dy, dx)
        send(packed.at[xx, yy], ret.at[j], arrivals + j // part, device(yy, z, xx))

    wait_recv(idx_all.at[pl.ds(0, (nx - 1) * ny)], 1)
    wait_recv(wsw_in, 3)
    wblock = wown.shape[0] // (nz * nx)
    wrs_out[...] = (wown + wsw_in[...].astype(F32)).astype(BF16).reshape(nz * nx, wblock, half_width)
    wrs_in[zx] = wrs_out[zx]
    for dz, dx in planes:
        zz, xx = in_plane(dz, dx)
        send(wrs_out.at[zz * nx + xx], wrs_in.at[zx], 4, device(y, zz, xx))

    half_rows = shard_rows // nc
    m = iota((16, nx * slots), 0)
    starts = [(z_ * nx + x_) * 32 for z_, x_ in [in_plane(*d) for d in planes + [(0, 0)]]]
    listed = jnp.concatenate([idx_all[j][:, :cap] for j in range(nx * ny)], axis=1)
    for s in range(2):
        side = 1 - core if s == 0 else core
        for g, start in enumerate(starts):
            hot[s, g * 16 : (g + 1) * 16] = (
                (m + (start + side * 16) == listed).astype(F32).astype(BF16)
            )

    sums = [None, None]
    for a in range(last):
        wait_recv(ret.at[pl.ds(0, part)], arrivals + a)
        block = ret[a * part : (a + 1) * part].reshape(part * cap, chunk)
        for s in range(2):
            term = dot(hot[s, :, a * part * cap : (a + 1) * part * cap], block)
            sums[s] = term if a == 0 else sums[s] + term

    wait_recv(wrs_in.at[pl.ds(0, nz * nx - 1)], 4)
    wsum = jnp.sum(wrs_in[...].astype(F32), axis=0)
    way_out[...] = wsum.astype(BF16)

    wait_recv(ret.at[pl.ds(0, part - 1)], arrivals + last)
    block = ret[last * part :].reshape(part * cap, chunk)
    pieces = [slice(0, half_rows // 2), slice(half_rows // 2, half_rows)]

    def piece_sum(s, piece):
        return sums[s][piece] + dot(hot[s, piece, last * part * cap :], block)

    for stage, piece in zip((6, 8), pieces):
        half_out[piece] = piece_sum(0, piece).astype(BF16)
        send(half_out.at[piece], half_in.at[piece], stage, sibling)
    way_in[y] = way_out[...]
    for dy in near:
        yy, _ = in_column(dy, 0)
        send(way_out, way_in.at[y], 5, device(yy, z, x))
    own = [piece_sum(1, piece) for piece in pieces]

    groups = nz * nx // 2
    for i, (stage, piece) in enumerate(zip((6, 8), pieces)):
        wait_recv(half_in.at[piece], stage)
        total = own[i] + half_in[piece].astype(F32)
        rs_out[i * groups : (i + 1) * groups] = total.astype(BF16).reshape(groups, 16, chunk)
        for g in range(i * groups, min((i + 1) * groups, own_plane)):
            zz, xx = in_plane(*planes[g])
            send(rs_out.at[g], rs_in.at[g], 9, device(y, zz, xx))
    rs_in[own_plane] = rs_out[own_plane]

    wait_recv(way_in.at[pl.ds(0, ny - 1)], 5)
    wsum = jnp.sum(way_in[...].astype(F32), axis=0)
    wrows = wblock // nc
    wsum = [wsum[c * wrows : (c + 1) * wrows] for c in range(2)]
    wfin_out[...] = jnp.where(core == 0, wsum[1], wsum[0])
    wown = jnp.where(core == 0, wsum[0], wsum[1])
    send(wfin_out, wfin_in, 7, sibling)

    wait_recv(wfin_in, 7)
    wother = wfin_in[...]
    wgrad_ref[:, :half_width] = jnp.where(core == 0, wown, wother).astype(BF16)
    wgrad_ref[:, half_width:] = jnp.where(core == 0, wother, wown).astype(BF16)
    for dy in near:
        wait_send(idx_own.at[pl.ds(0, 1)], lists + dy)
    wait_send(idx_all.at[pl.ds(0, (nx - 1) * ny)], 1)
    wait_send(fetched.at[pl.ds(0, ny - 1)], 2)
    wait_send(wsw_out, 3)
    wait_send(wrs_out.at[pl.ds(0, nz * nx - 1)], 4)
    wait_send(way_in.at[pl.ds(0, ny - 1)], 5)
    for a in range(parts_of):
        wait_send(ret.at[pl.ds(0, part - (a == last))], arrivals + a)
    wait_send(wfin_out, 7)
    for stage, piece in zip((6, 8), pieces):
        wait_send(half_out.at[piece], stage)
    store.wait()
    wait_recv(rs_in.at[pl.ds(0, nz * nx - 1)], 9)
    for dx in range(nx):
        acc = None
        for g, (dz, dx_) in enumerate(planes + [(0, 0)]):
            if dx_ == dx:
                term = rs_in[g].astype(F32)
                acc = term if acc is None else acc + term
        start = pl.multiple_of(((x - dx) & (nx - 1)) * chunk, chunk)
        tgrad_ref[:, pl.ds(start, chunk)] = acc
    wait_send(rs_out.at[pl.ds(0, nz * nx - 1)], 9)


def hand_on(*refs):
    given, results, held = refs[:3], refs[3:6], refs[6:9]
    in_sem, out_sem = refs[9:]
    ins = [pltpu.make_async_copy(given[i], held[i], in_sem.at[i]) for i in range(3)]
    outs = [pltpu.make_async_copy(held[i], results[i], out_sem.at[i]) for i in range(3)]
    for copy in ins:
        copy.start()
    for i in range(3):
        ins[i].wait()
        outs[i].start()
    for copy in outs:
        copy.wait()


def on_device(ny, nz, nx, cap, table, owner, local_row, lengths, w_in, w_out, cotangent):
    tok, width = cotangent.shape
    shard_rows = table.shape[0]
    chunk = width // nx
    slots = ny * cap
    nc = CORES
    wblock = width // (nz * nx)
    half_width = width // nc
    vmem = pl.BlockSpec(memory_space=pltpu.VMEM)
    anywhere = pl.BlockSpec(memory_space=pl.ANY)
    V = pltpu.VMEM
    scratch = [
        V((1, tok), jnp.int32),
        V((1, tok), jnp.int32),
        V(lengths.shape, jnp.int32),
        V(table.shape, BF16),
        V(w_in.shape, BF16),
        V(w_out.shape, BF16),
        V(cotangent.shape, BF16),
        V(cotangent.shape, BF16),
        V((ny, 1, -(-cap // 128) * 128), jnp.int32),
        V((nx * ny, 1, -(-cap // 128) * 128), jnp.int32),
        V((ny, cap, width), BF16),
        V((ny, cap, width), BF16),
        V((slots, tok), BF16),
        V((2, shard_rows // nc, nx * slots), BF16),
        V((4, tok, width), BF16),
        V((4, tok, width), F32),
        V((HEADS, tok, tok), BF16),
        V((HEADS, tok, tok), F32),
        V((3, tok, width), BF16),
        V((nx, ny, cap, chunk), BF16),
        V((nx * ny, cap, chunk), BF16),
        V((shard_rows // nc, chunk), BF16),
        V((shard_rows // nc, chunk), BF16),
        V((nz * nx, 16, chunk), BF16),
        V((nz * nx, 16, chunk), BF16),
        V((width, half_width), BF16),
        V((width, half_width), BF16),
        V((nz * nx, wblock, half_width), BF16),
        V((nz * nx, wblock, half_width), BF16),
        V((wblock, half_width), BF16),
        V((ny, wblock, half_width), BF16),
        V((wblock // nc, half_width), F32),
        V((wblock // nc, half_width), F32),
        pltpu.SemaphoreType.DMA((7,)),
        pltpu.SemaphoreType.DMA,
        pltpu.SemaphoreType.DMA((13 + ny,)),
        pltpu.SemaphoreType.DMA((13 + ny,)),
    ]
    results = pl.pallas_call(
        functools.partial(kernel, ny, nz, nx, cap),
        out_shape=(
            jax.ShapeDtypeStruct((tok, width), BF16),
            jax.ShapeDtypeStruct((shard_rows // (nz * nx * nc), width), F32),
            jax.ShapeDtypeStruct((wblock // nc, width), BF16),
        ),
        in_specs=[anywhere] * 7,
        out_specs=(anywhere, vmem, vmem),
        scratch_shapes=scratch,
        compiler_params=pltpu.CompilerParams(
            collective_id=0, has_side_effects=True, fuse_transposed_lhs_in_matmul=True, vmem_limit_bytes=56 * 1024 * 1024
        ),
        name="hstu",
    )(
        owner.reshape(1, tok),
        local_row.reshape(1, tok),
        lengths,
        table,
        w_in,
        w_out,
        cotangent,
    )
    return pl.pallas_call(
        hand_on,
        out_shape=tuple(jax.ShapeDtypeStruct(r.shape, r.dtype) for r in results),
        in_specs=[anywhere] * 3,
        out_specs=(anywhere,) * 3,
        scratch_shapes=[V(r.shape, r.dtype) for r in results]
        + [pltpu.SemaphoreType.DMA((3,)), pltpu.SemaphoreType.DMA((3,))],
        name="hand_on",
    )(*results)


def build(mesh, nx, cap):
    ny = mesh.shape["table"]
    nz = mesh.shape["batch"] // (nx * CORES)
    return jax.shard_map(
        functools.partial(on_device, ny, nz, nx, cap),
        mesh=mesh,
        in_specs=(
            P("table", None),
            P(("table", "batch"), None),
            P(("table", "batch")),
            P(("table", "batch"), None),
            P(),
            P(),
            P(("table", "batch"), None),
        ),
        out_specs=(P(("table", "batch"), None), P(("table", "batch"), None), P("batch", None)),
        check_vma=False,
    )


def solution(mesh):
    return build(mesh, 4, 48)
```

```python
import functools

import jax
import jax.numpy as jnp
from jax import lax
from jax.experimental import pallas as pl
from jax.experimental.pallas import tpu as pltpu
from jax.sharding import PartitionSpec as P

HEADS = 8
MOST_LEN = 192
EPSILON = 1e-05
CORES = 2
F32 = jnp.float32
BF16 = jnp.bfloat16


def dot(a, b):
    return lax.dot_general(a, b, (((1,), (0,)), ((), ())), preferred_element_type=F32)


def dot_nt(a, b):
    return lax.dot_general(a, b, (((1,), (1,)), ((), ())), preferred_element_type=F32)


def dot_tn(a, b):
    return lax.dot_general(a, b, (((0,), (0,)), ((), ())), preferred_element_type=F32)


def iota(shape, dim):
    return lax.broadcasted_iota(jnp.int32, shape, dim)


def sigmoid(z):
    return 0.5 * jnp.tanh(0.5 * z) + 0.5


def far_first(n):
    return sorted(range(n), key=lambda d: -min(d, n - d))


def kernel(
    ny, nz, nx, cap,
    owner_hbm, row_hbm, len_hbm, table_hbm, w_in_hbm, w_out_hbm, cot_hbm,
    out_hbm, tgrad_ref, wgrad_ref,
    owner_ref, row_ref, len_ref, table, w_in, w_out, cot, out,
    idx_own, idx_all, reply, fetched, place, hot,
    branch, slope, weight, sslope, sides,
    packed, ret, half_out, half_in, rs_out, rs_in,
    wsw_out, wsw_in, wrs_out, wrs_in, way_out, way_in, wfin_out, wfin_in,
    load_sem, store_sem, send_sem, recv_sem,
):
    tok, width = cot.shape
    nc = CORES
    pair_width = 128
    pairs = width // pair_width
    chunk = width // nx
    half_width = width // nc
    slots = ny * cap
    listed_width = idx_own.shape[-1]
    y = lax.axis_index("table")
    b = lax.axis_index("batch")
    core = b % nc
    x = (b // nc) % nx
    z = b // (nc * nx)
    zx = z * nx + x
    sibling = {"table": y, "batch": zx * nc + (1 - core)}

    def device(yy, zz, xx):
        return {"table": yy, "batch": (zz * nx + xx) * nc + core}

    columns = [(dy, dx) for dy in far_first(ny) for dx in far_first(nx) if (dy, dx) != (0, 0)]
    planes = [(dz, dx) for dz in far_first(nz) for dx in far_first(nx) if (dz, dx) != (0, 0)]

    own_column, own_plane = len(columns), len(planes)

    def in_column(dy, dx):
        return (y + dy) & (ny - 1), (x + dx) & (nx - 1)

    def in_plane(dz, dx):
        return (z + dz) & (nz - 1), (x + dx) & (nx - 1)

    loads = [
        pltpu.make_async_copy(src, dst, load_sem.at[i])
        for i, (src, dst) in enumerate(
            [
                (owner_hbm, owner_ref),
                (row_hbm, row_ref),
                (table_hbm, table),
                (len_hbm, len_ref),
                (cot_hbm, cot),
                (w_out_hbm, w_out),
                (w_in_hbm, w_in),
            ]
        )
    ]
    for load in loads[:2]:
        load.start()

    barrier = pltpu.get_barrier_semaphore()
    greeted = 0
    axes = (
        [device((y + d) & (ny - 1), z, x) for d in far_first(ny) if d]
        + [device(y, (z + d) & (nz - 1), x) for d in far_first(nz) if d]
        + [device(y, z, (x + d) & (nx - 1)) for d in far_first(nx) if d]
    )
    for target in axes:
        pl.semaphore_signal(barrier, inc=1, device_id=target)
        greeted += 1
    pl.semaphore_signal(barrier, inc=1, device_id=sibling)
    greeted += 1

    for load in loads[2:]:
        load.start()

    loads[0].wait()
    loads[1].wait()
    owner = owner_ref[...]
    rows = row_ref[...]
    mine = (iota((ny, tok), 0) == owner).astype(F32)
    earlier = (iota((tok, tok), 0) < iota((tok, tok), 1)).astype(F32).astype(BF16)
    before = dot(mine.astype(BF16), earlier)
    rank = jnp.sum(mine * before, axis=0, keepdims=True).astype(jnp.int32)
    rank_hot = (iota((listed_width, tok), 0) == rank).astype(F32).astype(BF16)
    high = (rows // 32).astype(F32)
    low = (rows % 32).astype(F32)
    parts = jnp.concatenate([mine * high, mine * low], axis=0).astype(BF16)
    listed = dot_nt(parts, rank_hot)
    listed = (listed[:ny] * 32.0 + listed[ny:]).astype(jnp.int32)
    for o in range(ny):
        idx_own[o] = listed[o : o + 1]
    idx_all[own_column] = idx_own[y]

    pl.semaphore_wait(barrier, greeted)

    def send(src, dst, stage, target):
        copy = pltpu.make_async_remote_copy(
            src_ref=src,
            dst_ref=dst,
            send_sem=send_sem.at[stage],
            recv_sem=recv_sem.at[stage],
            device_id=target,
        )
        copy.start()

    def wait_recv(slab, stage):
        pltpu.make_async_copy(slab, slab, recv_sem.at[stage]).wait()

    def wait_send(slab, stage):
        pltpu.make_async_copy(slab, slab, send_sem.at[stage]).wait()

    near = [dy for dy in far_first(ny) if dy]
    lists = 13
    for dy in near:
        yy, _ = in_column(dy, 0)
        send(idx_own.at[yy], idx_all.at[columns.index((dy, 0))], lists + dy, device(yy, z, x))
    loads[2].wait()

    order = near[::-1] + [0]
    shard_rows = table.shape[0]
    group = 2
    for first in range(0, ny, group):
        turn = order[first : first + group]
        for dy in turn:
            if dy:
                wait_recv(idx_all.at[pl.ds(0, 1)], lists + dy)
        asked = [idx_all[columns.index((dy, 0)) if dy else own_column] for dy in turn]
        asked = jnp.concatenate(asked * (8 // group), axis=0).astype(F32).T.astype(jnp.int32)
        picks = jnp.concatenate(
            [iota((cap, shard_rows), 1) == asked[:cap, k : k + 1] for k in range(group)], axis=0
        )
        found = dot(picks.astype(F32).astype(BF16), table[...]).astype(BF16)
        for k, dy in enumerate(turn):
            block = found[k * cap : (k + 1) * cap]
            if dy == 0:
                fetched[y] = block
            else:
                reply[dy] = block
                yy, _ = in_column(-dy, 0)
                send(reply.at[dy], fetched.at[y], 2, device(yy, z, x))

    for j, (dy, dx) in enumerate(columns):
        if dx:
            yy, xx = in_column(dy, dx)
            send(idx_own.at[yy], idx_all.at[j], 1, device(yy, z, xx))

    slot = owner * cap + rank
    place[...] = (iota((slots, tok), 0) == slot).astype(F32).astype(BF16)
    slot_col = jnp.broadcast_to(slot.astype(F32), (8, tok)).T[:, :1].astype(jnp.int32)
    unplace = (iota((tok, slots), 1) == slot_col).astype(F32).astype(BF16)
    loads[3].wait()
    loads[4].wait()
    loads[5].wait()
    dg = dot_nt(cot[...], w_out[...]).astype(BF16).astype(F32)
    bound = len_ref[:, :1]
    place_i = iota((tok, tok), 0)
    place_j = iota((tok, tok), 1)
    allowed = ((place_i >= bound) == (place_j >= bound)) & (place_j <= place_i)
    mask = jnp.where(allowed, 1.0 / MOST_LEN, 0.0).astype(F32)
    loads[6].wait()

    wait_recv(fetched.at[pl.ds(0, ny - 1)], 2)

    embedded = dot(unplace, fetched[...].reshape(slots, width)).astype(BF16)
    embedded = embedded.astype(F32)
    center = jnp.mean(embedded, axis=-1, keepdims=True)
    shifted = embedded - center
    scale = lax.rsqrt(jnp.mean(shifted * shifted, axis=-1, keepdims=True) + EPSILON)
    normed = shifted * scale
    normed_b = normed.astype(BF16)
    for i in range(4):
        hidden = dot(normed_b, w_in[:, i * width : (i + 1) * width])
        sig = sigmoid(hidden)
        value = hidden * sig
        branch[i] = value.astype(BF16)
        slope[i] = sig + value * (1.0 - sig)

    first_lane = iota((tok, pair_width), 1) < width // HEADS
    halves = [(0, tok // 2, tok // 2), (tok // 2, tok, tok)]

    def split(values):
        zero = jnp.zeros_like(values)
        return jnp.where(first_lane, values, zero), jnp.where(first_lane, zero, values)

    attended = []
    for p in range(pairs):
        lanes = slice(p * pair_width, (p + 1) * pair_width)
        v = split(branch[1, :, lanes])
        q = split(branch[2, :, lanes] * BF16(0.125))
        k = branch[3, :, lanes]
        result = []
        for lo, hi, js in halves:
            total = None
            for h in range(2):
                score = dot_nt(q[h][lo:hi], k[:js])
                sig = sigmoid(score)
                value = score * sig
                m = mask[lo:hi, :js]
                w = (value * m).astype(BF16)
                weight[2 * p + h, lo:hi, :js] = w
                sslope[2 * p + h, lo:hi, :js] = (sig + value * (1.0 - sig)) * m
                term = dot(w, v[h][:js])
                total = term if total is None else total + term
            result.append(total)
        attended.append(jnp.concatenate(result, axis=0))
    attended = jnp.concatenate(attended, axis=1)
    center2 = jnp.mean(attended, axis=-1, keepdims=True)
    shifted2 = attended - center2
    scale2 = lax.rsqrt(jnp.mean(shifted2 * shifted2, axis=-1, keepdims=True) + EPSILON)
    normed2 = shifted2 * scale2
    gate = branch[0].astype(F32)
    gated = (normed2 * gate).astype(BF16)

    wgrad = dot_tn(gated, cot[...])
    wgrad = [wgrad[:, c * half_width : (c + 1) * half_width] for c in range(2)]
    wsw_out[...] = jnp.where(core == 0, wgrad[1], wgrad[0]).astype(BF16)
    wown = jnp.where(core == 0, wgrad[0], wgrad[1])
    send(wsw_out, wsw_in, 3, sibling)

    out[...] = (dot(gated, w_out[...]) + embedded).astype(BF16)
    store = pltpu.make_async_copy(out, out_hbm, store_sem)
    store.start()

    d_n2 = dg * gate
    d_gate = (dg * normed2).astype(BF16).astype(F32)
    d_att = scale2 * (
        d_n2
        - jnp.mean(d_n2, axis=-1, keepdims=True)
        - normed2 * jnp.mean(d_n2 * normed2, axis=-1, keepdims=True)
    )
    d_att = d_att.astype(BF16)
    d_normed = dot_nt((d_gate * slope[0]).astype(BF16), w_in[:, :width])

    for p in range(pairs):
        lanes = slice(p * pair_width, (p + 1) * pair_width)
        d_o = split(d_att[:, lanes])
        q = split(branch[2, :, lanes] * BF16(0.125))
        k = split(branch[3, :, lanes])
        v = branch[1, :, lanes]
        half = tok // 2
        dv_low = dv_all = dk_low = dk_all = None
        dq = []
        for lo, hi, js in halves:
            dq_sum = None
            for h in range(2):
                d_w = dot_nt(d_o[h][lo:hi], v[:js])
                d_s = (d_w * sslope[2 * p + h, lo:hi, :js]).astype(BF16)
                term = dot(d_s, k[h][:js])
                dq_sum = term if dq_sum is None else dq_sum + term
                dk = dot_tn(d_s, q[h][lo:hi])
                dv = dot_tn(weight[2 * p + h, lo:hi, :js], d_o[h][lo:hi])
                if lo == 0:
                    dk_low = dk if dk_low is None else dk_low + dk
                    dv_low = dv if dv_low is None else dv_low + dv
                else:
                    dk_all = dk if dk_all is None else dk_all + dk
                    dv_all = dv if dv_all is None else dv_all + dv
            dq.append(dq_sum * 0.125)
        dq = jnp.concatenate(dq, axis=0)
        dk = jnp.concatenate([dk_all[:half] + dk_low, dk_all[half:]], axis=0)
        dv = jnp.concatenate([dv_all[:half] + dv_low, dv_all[half:]], axis=0)
        for i, value in ((1, dv), (2, dq), (3, dk)):
            value = value.astype(BF16).astype(F32)
            sides[i - 1, :, lanes] = (value * slope[i, :, lanes]).astype(BF16)

    for i in range(1, 4):
        d_normed = d_normed + dot_nt(sides[i - 1], w_in[:, i * width : (i + 1) * width])
    d_normed = d_normed.astype(BF16).astype(F32)
    d_emb = scale * (
        d_normed
        - jnp.mean(d_normed, axis=-1, keepdims=True)
        - normed * jnp.mean(d_normed * normed, axis=-1, keepdims=True)
    )
    token_grads = (d_emb + cot[...].astype(F32)).astype(BF16)

    parts_of = 4 if nx * ny >= 8 else 2
    part = nx * ny // parts_of
    last = parts_of - 1
    arrivals = 10
    spread = dot(place[...], token_grads).astype(BF16)
    for xx in range(nx):
        packed[xx] = spread[:, xx * chunk : (xx + 1) * chunk].reshape(ny, cap, chunk)
    ret[own_column] = packed[x, y]
    for j, (dy, dx) in enumerate(columns):
        yy, xx = in_column(dy, dx)
        send(packed.at[xx, yy], ret.at[j], arrivals + j // part, device(yy, z, xx))

    wait_recv(idx_all.at[pl.ds(0, (nx - 1) * ny)], 1)
    wait_recv(wsw_in, 3)
    wblock = wown.shape[0] // (nz * nx)
    wrs_out[...] = (wown + wsw_in[...].astype(F32)).astype(BF16).reshape(nz * nx, wblock, half_width)
    wrs_in[zx] = wrs_out[zx]
    for dz, dx in planes:
        zz, xx = in_plane(dz, dx)
        send(wrs_out.at[zz * nx + xx], wrs_in.at[zx], 4, device(y, zz, xx))

    half_rows = shard_rows // nc
    m = iota((16, nx * slots), 0)
    starts = [(z_ * nx + x_) * 32 for z_, x_ in [in_plane(*d) for d in planes + [(0, 0)]]]
    listed = jnp.concatenate([idx_all[j][:, :cap] for j in range(nx * ny)], axis=1)
    for s in range(2):
        side = 1 - core if s == 0 else core
        for g, start in enumerate(starts):
            hot[s, g * 16 : (g + 1) * 16] = (
                (m + (start + side * 16) == listed).astype(F32).astype(BF16)
            )

    sums = [None, None]
    for a in range(last):
        wait_recv(ret.at[pl.ds(0, part)], arrivals + a)
        block = ret[a * part : (a + 1) * part].reshape(part * cap, chunk)
        for s in range(2):
            term = dot(hot[s, :, a * part * cap : (a + 1) * part * cap], block)
            sums[s] = term if a == 0 else sums[s] + term

    wait_recv(wrs_in.at[pl.ds(0, nz * nx - 1)], 4)
    wsum = jnp.sum(wrs_in[...].astype(F32), axis=0)
    way_out[...] = wsum.astype(BF16)

    wait_recv(ret.at[pl.ds(0, part - 1)], arrivals + last)
    block = ret[last * part :].reshape(part * cap, chunk)
    pieces = [slice(0, half_rows // 2), slice(half_rows // 2, half_rows)]

    def piece_sum(s, piece):
        return sums[s][piece] + dot(hot[s, piece, last * part * cap :], block)

    for stage, piece in zip((6, 8), pieces):
        half_out[piece] = piece_sum(0, piece).astype(BF16)
        send(half_out.at[piece], half_in.at[piece], stage, sibling)
    way_in[y] = way_out[...]
    for dy in near:
        yy, _ = in_column(dy, 0)
        send(way_out, way_in.at[y], 5, device(yy, z, x))
    own = [piece_sum(1, piece) for piece in pieces]

    groups = nz * nx // 2
    for i, (stage, piece) in enumerate(zip((6, 8), pieces)):
        wait_recv(half_in.at[piece], stage)
        total = own[i] + half_in[piece].astype(F32)
        rs_out[i * groups : (i + 1) * groups] = total.astype(BF16).reshape(groups, 16, chunk)
        for g in range(i * groups, min((i + 1) * groups, own_plane)):
            zz, xx = in_plane(*planes[g])
            send(rs_out.at[g], rs_in.at[g], 9, device(y, zz, xx))
    rs_in[own_plane] = rs_out[own_plane]

    wait_recv(way_in.at[pl.ds(0, ny - 1)], 5)
    wsum = jnp.sum(way_in[...].astype(F32), axis=0)
    wrows = wblock // nc
    wsum = [wsum[c * wrows : (c + 1) * wrows] for c in range(2)]
    wfin_out[...] = jnp.where(core == 0, wsum[1], wsum[0])
    wown = jnp.where(core == 0, wsum[0], wsum[1])
    send(wfin_out, wfin_in, 7, sibling)

    wait_recv(wfin_in, 7)
    wother = wfin_in[...]
    wgrad_ref[:, :half_width] = jnp.where(core == 0, wown, wother).astype(BF16)
    wgrad_ref[:, half_width:] = jnp.where(core == 0, wother, wown).astype(BF16)
    for dy in near:
        wait_send(idx_own.at[pl.ds(0, 1)], lists + dy)
    wait_send(idx_all.at[pl.ds(0, (nx - 1) * ny)], 1)
    wait_send(fetched.at[pl.ds(0, ny - 1)], 2)
    wait_send(wsw_out, 3)
    wait_send(wrs_out.at[pl.ds(0, nz * nx - 1)], 4)
    wait_send(way_in.at[pl.ds(0, ny - 1)], 5)
    for a in range(parts_of):
        wait_send(ret.at[pl.ds(0, part - (a == last))], arrivals + a)
    wait_send(wfin_out, 7)
    for stage, piece in zip((6, 8), pieces):
        wait_send(half_out.at[piece], stage)
    store.wait()
    wait_recv(rs_in.at[pl.ds(0, nz * nx - 1)], 9)
    for dx in range(nx):
        acc = None
        for g, (dz, dx_) in enumerate(planes + [(0, 0)]):
            if dx_ == dx:
                term = rs_in[g].astype(F32)
                acc = term if acc is None else acc + term
        start = pl.multiple_of(((x - dx) & (nx - 1)) * chunk, chunk)
        tgrad_ref[:, pl.ds(start, chunk)] = acc
    wait_send(rs_out.at[pl.ds(0, nz * nx - 1)], 9)


def hand_on(*refs):
    given, results, held = refs[:3], refs[3:6], refs[6:9]
    in_sem, out_sem = refs[9:]
    ins = [pltpu.make_async_copy(given[i], held[i], in_sem.at[i]) for i in range(3)]
    outs = [pltpu.make_async_copy(held[i], results[i], out_sem.at[i]) for i in range(3)]
    for copy in ins:
        copy.start()
    for i in range(3):
        ins[i].wait()
        outs[i].start()
    for copy in outs:
        copy.wait()


def on_device(ny, nz, nx, cap, table, owner, local_row, lengths, w_in, w_out, cotangent):
    tok, width = cotangent.shape
    shard_rows = table.shape[0]
    chunk = width // nx
    slots = ny * cap
    nc = CORES
    wblock = width // (nz * nx)
    half_width = width // nc
    vmem = pl.BlockSpec(memory_space=pltpu.VMEM)
    anywhere = pl.BlockSpec(memory_space=pl.ANY)
    V = pltpu.VMEM
    scratch = [
        V((1, tok), jnp.int32),
        V((1, tok), jnp.int32),
        V(lengths.shape, jnp.int32),
        V(table.shape, BF16),
        V(w_in.shape, BF16),
        V(w_out.shape, BF16),
        V(cotangent.shape, BF16),
        V(cotangent.shape, BF16),
        V((ny, 1, -(-cap // 128) * 128), jnp.int32),
        V((nx * ny, 1, -(-cap // 128) * 128), jnp.int32),
        V((ny, cap, width), BF16),
        V((ny, cap, width), BF16),
        V((slots, tok), BF16),
        V((2, shard_rows // nc, nx * slots), BF16),
        V((4, tok, width), BF16),
        V((4, tok, width), F32),
        V((HEADS, tok, tok), BF16),
        V((HEADS, tok, tok), F32),
        V((3, tok, width), BF16),
        V((nx, ny, cap, chunk), BF16),
        V((nx * ny, cap, chunk), BF16),
        V((shard_rows // nc, chunk), BF16),
        V((shard_rows // nc, chunk), BF16),
        V((nz * nx, 16, chunk), BF16),
        V((nz * nx, 16, chunk), BF16),
        V((width, half_width), BF16),
        V((width, half_width), BF16),
        V((nz * nx, wblock, half_width), BF16),
        V((nz * nx, wblock, half_width), BF16),
        V((wblock, half_width), BF16),
        V((ny, wblock, half_width), BF16),
        V((wblock // nc, half_width), F32),
        V((wblock // nc, half_width), F32),
        pltpu.SemaphoreType.DMA((7,)),
        pltpu.SemaphoreType.DMA,
        pltpu.SemaphoreType.DMA((13 + ny,)),
        pltpu.SemaphoreType.DMA((13 + ny,)),
    ]
    results = pl.pallas_call(
        functools.partial(kernel, ny, nz, nx, cap),
        out_shape=(
            jax.ShapeDtypeStruct((tok, width), BF16),
            jax.ShapeDtypeStruct((shard_rows // (nz * nx * nc), width), F32),
            jax.ShapeDtypeStruct((wblock // nc, width), BF16),
        ),
        in_specs=[anywhere] * 7,
        out_specs=(anywhere, vmem, vmem),
        scratch_shapes=scratch,
        compiler_params=pltpu.CompilerParams(
            collective_id=0, has_side_effects=True, fuse_transposed_lhs_in_matmul=True, vmem_limit_bytes=56 * 1024 * 1024
        ),
        name="hstu",
    )(
        owner.reshape(1, tok),
        local_row.reshape(1, tok),
        lengths,
        table,
        w_in,
        w_out,
        cotangent,
    )
    return pl.pallas_call(
        hand_on,
        out_shape=tuple(jax.ShapeDtypeStruct(r.shape, r.dtype) for r in results),
        in_specs=[anywhere] * 3,
        out_specs=(anywhere,) * 3,
        scratch_shapes=[V(r.shape, r.dtype) for r in results]
        + [pltpu.SemaphoreType.DMA((3,)), pltpu.SemaphoreType.DMA((3,))],
        name="hand_on",
    )(*results)


def build(mesh, nx, cap):
    ny = mesh.shape["table"]
    nz = mesh.shape["batch"] // (nx * CORES)
    return jax.shard_map(
        functools.partial(on_device, ny, nz, nx, cap),
        mesh=mesh,
        in_specs=(
            P("table", None),
            P(("table", "batch"), None),
            P(("table", "batch")),
            P(("table", "batch"), None),
            P(),
            P(),
            P(("table", "batch"), None),
        ),
        out_specs=(P(("table", "batch"), None), P(("table", "batch"), None), P("batch", None)),
        check_vma=False,
    )


def solution(mesh):
    return build(mesh, 4, 48)
```
